512 devices in a mesh: seq: 64 (over z, x_lo, core), tp: 8 (over x_hi, y).
Axes of the slice: x: 4 (x_hi: 2, x_lo: 2; x = x_hi * 2 + x_lo), y: 4, z: 16, core: 2. Of those that a mesh axis runs over, the one named last changes fastest.
Arguments:
- query: bfloat16 [4096, 4096], P(('seq', 'tp')), may hold values from -150 to 150
- key_new: bfloat16 [4096, 1024], P(('seq', 'tp')), may hold values from -5 to 5
- value_new: bfloat16 [4096, 1024], P(('seq', 'tp')), may hold values from -6 to 6
- ssm_input: bfloat16 [4096, 8192], P(('seq', 'tp')), may hold values from -6 to 6
- ssm_gate: bfloat16 [4096, 8192], P(('seq', 'tp')), may hold values from -6 to 6
- ssm_b: bfloat16 [4096, 1024], P(('seq', 'tp')), may hold values from -4 to 4
- ssm_c: bfloat16 [4096, 1024], P(('seq', 'tp')), may hold values from -4 to 4
- log_decay: bfloat16 [4096, 128], P(('seq', 'tp')), may hold values from -0.8 to 0
- key_cache: bfloat16 [4096, 1024], P('seq', 'tp'), may hold values from -6 to 6
- value_cache: bfloat16 [4096, 1024], P('seq', 'tp'), may hold values from -6 to 6
- init_state: float32 [128, 64, 128], P('tp'), may hold values from -4 to 4
- skip_gain: float32 [128], P('tp'), may hold values from 0.3 to 1.5
- norm_gain: float32 [8192], P('tp'), may hold values from 0.5 to 1.5
- cache_length: int32 [1], replicated, may hold values from 1 to 4096
- span_start: int32 [1], replicated, may hold values from 0 to 255
Outputs:
- attn_output: bfloat16 [4096, 4096], P(('seq', 'tp'))
- ssm_output: bfloat16 [4096, 8192], P(('seq', 'tp'))
The draws below stay inside these ranges and needn't reach their ends.
All inputs are finite; a program needn't handle non-finite values.
Results may differ from the reference program's by a relative error of at most 0.0095.
Values may be sent and summed in bfloat16 or wider, within the bound.
A program may use at most 128 MiB of HBM per device.

```python
import math
import jax
import jax.numpy as jnp
from jax import lax

HQ = 32
HK = 8
DH = 128
SSM_CHANNEL_COUNT = 128
P_SIZE = 64
N = 128
G = 8
WINDOW_LENGTH = 4096
CACHE = 4096


def shared_rows(key):
    base_keys = jax.random.truncated_normal(jax.random.fold_in(key, 101), -4.0, 4.0, (WINDOW_LENGTH, HK * DH), jnp.float32)
    return base_keys


def draw_key_new(key, part):
    base_keys = shared_rows(key)
    return base_keys.astype(jnp.bfloat16)


def draw_query(key, part):
    key = jax.random.fold_in(key, 5)
    queries = jax.random.truncated_normal(key, -4.0, 4.0, (WINDOW_LENGTH, HQ * DH), jnp.float32)
    return queries.astype(jnp.bfloat16)


def draw_log_decay(key, part):
    key = jax.random.fold_in(key, 7)
    key_fast, key_quick, key_slow, key_rough, lookup_locations, lookup_fading_penalty = jax.random.split(key, 6)
    fast_share = 0.5
    is_fast = jax.random.uniform(key_fast, (SSM_CHANNEL_COUNT,), jnp.float32) < fast_share
    quick_rate = jax.random.uniform(key_quick, (SSM_CHANNEL_COUNT,), jnp.float32, 1.0 / 50.0, 1.0 / 30.0)
    slow_rate = jnp.exp(jax.random.uniform(key_slow, (SSM_CHANNEL_COUNT,), jnp.float32, math.log(0.02), math.log(0.3))) * (math.log(10.0) / WINDOW_LENGTH / 1.25)
    channel_fading_speed = jnp.where(is_fast, quick_rate, slow_rate)
    noise_magnitude = jax.random.uniform(key_rough, (WINDOW_LENGTH, SSM_CHANNEL_COUNT), jnp.float32, 0.5, 2.0)
    spike_locations = jax.random.randint(lookup_locations, (2,), 0, WINDOW_LENGTH)
    spike_fading_penalty = jax.random.uniform(lookup_fading_penalty, (2, SSM_CHANNEL_COUNT), jnp.float32, 0.2, 0.5)
    sequence_locations = jnp.arange(WINDOW_LENGTH, dtype=jnp.int32)
    earliest_spike_place = jnp.where((sequence_locations == spike_locations[0])[:, None], -jnp.log(1.0 - spike_fading_penalty[0])[None, :], 0.0)
    latter_spike_place = jnp.where((sequence_locations == spike_locations[1])[:, None], -jnp.log(1.0 - spike_fading_penalty[1])[None, :], 0.0)
    fading_exponent_amount = -(channel_fading_speed[None, :] * noise_magnitude) - earliest_spike_place - latter_spike_place
    return fading_exponent_amount.astype(jnp.bfloat16)


def steps_of(rng, shape, cuts, low, largest):
    def one(dim, shards_of):
        draws = jax.random.uniform(jax.random.fold_in(jax.random.fold_in(rng, 6), dim), (shards_of,), jnp.float32, low / len(cuts), largest / len(cuts))
        return jnp.repeat(jnp.exp(draws), shape[dim] // shards_of).reshape((-1,) + (1,) * (len(shape) - dim - 1))

    gain = one(*cuts[0])
    for cut in cuts[1:]:
        gain = gain * one(*cut)
    return gain


def normal_values(stream_key, dims, deviation, reach, shards=(), kind=jnp.bfloat16):
    result = deviation * jax.random.normal(stream_key, dims, jnp.float32)
    if shards:
        result = result * steps_of(stream_key, dims, shards, -0.22, 0.18)
    return jnp.clip(result, -reach, reach).astype(kind)


def setup_inputs(seed: int = 0) -> dict:
    streams_of = jax.random.split(jax.random.key(seed), 16)
    query = draw_query(jax.random.fold_in(streams_of[15], 71), 0)
    key_new = draw_key_new(jax.random.fold_in(streams_of[15], 71), 0)
    value_new = normal_values(streams_of[2], (WINDOW_LENGTH, HK * DH), 1.0, 6.0, ((0, 512),))
    ssm_input = normal_values(streams_of[3], (WINDOW_LENGTH, SSM_CHANNEL_COUNT * P_SIZE), 1.0, 6.0, ((0, 512),))
    ssm_gate = normal_values(streams_of[4], (WINDOW_LENGTH, SSM_CHANNEL_COUNT * P_SIZE), 1.0, 6.0, ((0, 512),))
    ssm_b = normal_values(streams_of[5], (WINDOW_LENGTH, G * N), 0.3, 4.0, ((0, 512),))
    ssm_c = normal_values(streams_of[6], (WINDOW_LENGTH, G * N), 0.3, 4.0, ((0, 512),))
    log_decay = draw_log_decay(jax.random.fold_in(streams_of[15], 71), 0)
    key_cache = normal_values(streams_of[8], (CACHE, HK * DH), 1.0, 6.0, ((0, 64), (1, 8)))
    value_cache = normal_values(streams_of[9], (CACHE, HK * DH), 1.0, 6.0, ((0, 64), (1, 8)))
    init_state = normal_values(streams_of[10], (SSM_CHANNEL_COUNT, P_SIZE, N), 0.3, 4.0, ((0, 8),), jnp.float32)
    skip_gain = jnp.clip(jnp.exp(math.log(1.5) - 1.60943787 * jax.random.uniform(streams_of[11], (SSM_CHANNEL_COUNT,), jnp.float32) ** steps_of(streams_of[11], (SSM_CHANNEL_COUNT,), ((0, 8),), -0.2, 0.2)), 0.3, 1.5)
    norm_gain = jnp.clip(1.0 + 0.1 * jax.random.normal(streams_of[12], (SSM_CHANNEL_COUNT * P_SIZE,), jnp.float32), 0.5, 1.5)
    cache_length = jax.random.randint(streams_of[13], (1,), 1, CACHE + 1).astype(jnp.int32)
    span_start = jax.random.randint(streams_of[14], (1,), 0, WINDOW_LENGTH // 16).astype(jnp.int32)
    return dict(query=query, key_new=key_new, value_new=value_new, ssm_input=ssm_input, ssm_gate=ssm_gate, ssm_b=ssm_b, ssm_c=ssm_c, log_decay=log_decay, key_cache=key_cache, value_cache=value_cache, init_state=init_state, skip_gain=skip_gain, norm_gain=norm_gain, cache_length=cache_length, span_start=span_start)


def attention_part(query, key_new, value_new, key_cache, value_cache, cache_length, span_start):
    ratio_heads = HQ // HK
    score_scale = 1.0 / math.sqrt(DH)
    block_rows = math.gcd(WINDOW_LENGTH, 1024)
    block_count = WINDOW_LENGTH // block_rows
    cache_places = jnp.arange(CACHE, dtype=jnp.int32)
    span_places = jnp.arange(WINDOW_LENGTH, dtype=jnp.int32)
    cache_usable = cache_places < cache_length[0]
    results = []
    for kv_head in range(HK):
        key_rows = jnp.concatenate([key_cache[:, kv_head * DH:(kv_head + 1) * DH], key_new[:, kv_head * DH:(kv_head + 1) * DH]], 0).astype(jnp.float32)
        value_rows = jnp.concatenate([value_cache[:, kv_head * DH:(kv_head + 1) * DH], value_new[:, kv_head * DH:(kv_head + 1) * DH]], 0).astype(jnp.float32)
        head_queries = query[:, kv_head * ratio_heads * DH:(kv_head + 1) * ratio_heads * DH].reshape(block_count, block_rows, ratio_heads, DH)

        def one_block(block_args):
            query_rows, first_row = block_args
            query_places = first_row + jnp.arange(block_rows, dtype=jnp.int32)
            span_usable = (span_places[None, :] >= span_start[0]) & (span_places[None, :] <= query_places[:, None])
            usable = jnp.concatenate([jnp.broadcast_to(cache_usable[None, :], (block_rows, CACHE)), span_usable], 1)
            scores = jnp.einsum('trd,sd->rts', query_rows.astype(jnp.float32), key_rows) * score_scale
            scores = jnp.where(usable[None], scores, -1e+30)
            row_top = lax.optimization_barrier(jnp.max(scores, axis=-1))
            weights = jnp.where(usable[None], jnp.exp(scores - row_top[..., None]), 0.0)
            weight_sum = lax.optimization_barrier(jnp.sum(weights, axis=-1))
            rounded = weights.astype(jnp.bfloat16).astype(jnp.float32)
            mixed = jnp.einsum('rts,sd->trd', rounded, value_rows)
            return (mixed / jnp.transpose(weight_sum)[:, :, None]).astype(jnp.bfloat16)
        first_rows = jnp.arange(block_count, dtype=jnp.int32) * block_rows
        head_out = lax.map(one_block, (head_queries, first_rows))
        results.append(head_out.reshape(WINDOW_LENGTH, ratio_heads * DH))
    return jnp.concatenate(results, 1)

def ssm_part(ssm_input, ssm_gate, ssm_b, ssm_c, log_decay, init_state, skip_gain, norm_gain, span_start):
    block_rows = math.gcd(WINDOW_LENGTH, 256)
    block_count = WINDOW_LENGTH // block_rows
    per_group = SSM_CHANNEL_COUNT // G
    highest = lax.Precision.HIGHEST
    inputs_all = ssm_input.reshape(block_count, block_rows, SSM_CHANNEL_COUNT, P_SIZE)
    b_all = ssm_b.reshape(block_count, block_rows, G, N)
    c_all = ssm_c.reshape(block_count, block_rows, G, N)
    decay_all = log_decay.reshape(block_count, block_rows, SSM_CHANNEL_COUNT)
    first_rows = jnp.arange(block_count, dtype=jnp.int32) * block_rows
    row_index = jnp.arange(block_rows, dtype=jnp.int32)
    lower_mask = row_index[:, None] >= row_index[None, :]

    def one_block(carried, block_args):
        input_raw, b_raw, c_raw, decay_raw, first_row = block_args
        sequence_locations = first_row + row_index
        fading_exponent_amount = jnp.where(sequence_locations[:, None] >= span_start[0], decay_raw.astype(jnp.float32), 0.0)
        in_weight = jnp.sqrt(-jnp.expm1(2.0 * fading_exponent_amount))
        cum_decay = jnp.cumsum(fading_exponent_amount, axis=0)
        weighted = input_raw.astype(jnp.float32) * in_weight[:, :, None]
        b_spread = jnp.repeat(b_raw.astype(jnp.float32), per_group, axis=1)
        c_spread = jnp.repeat(c_raw.astype(jnp.float32), per_group, axis=1)
        pair_score = jnp.einsum('tgn,sgn->gts', c_raw.astype(jnp.float32), b_raw.astype(jnp.float32))
        pair_score = jnp.repeat(pair_score, per_group, axis=0)
        cum_heads = jnp.transpose(cum_decay)
        gaps = cum_heads[:, :, None] - cum_heads[:, None, :]
        gap_decay = jnp.where(lower_mask[None], jnp.exp(jnp.where(lower_mask[None], gaps, 0.0)), 0.0)
        ssm_y = jnp.einsum('hts,shp->thp', pair_score * gap_decay, weighted, precision=highest)
        ssm_y = ssm_y + jnp.exp(cum_decay)[:, :, None] * jnp.einsum('thn,hpn->thp', c_spread, carried, precision=highest)
        ssm_y = ssm_y + skip_gain[None, :, None] * input_raw.astype(jnp.float32)
        end_log = cum_decay[-1]
        to_end = jnp.exp(end_log[None, :] - cum_decay)
        fresh = jnp.einsum('sh,shp,shn->hpn', to_end, weighted, b_spread, precision=highest)
        carried = jnp.exp(end_log)[:, None, None] * carried + fresh
        return (carried, ssm_y)
    final_state, ys_all = lax.scan(one_block, init_state, (inputs_all, b_all, c_all, decay_all, first_rows))
    ssm_y = ys_all.reshape(WINDOW_LENGTH, SSM_CHANNEL_COUNT, P_SIZE)
    gated_y = ssm_y * jax.nn.silu(ssm_gate.reshape(WINDOW_LENGTH, SSM_CHANNEL_COUNT, P_SIZE).astype(jnp.float32))
    grouped = gated_y.reshape(WINDOW_LENGTH, G, per_group * P_SIZE)
    mean_sq = lax.optimization_barrier(jnp.mean(grouped * grouped, axis=-1, keepdims=True))
    normed = grouped * lax.rsqrt(mean_sq + 1e-05) * norm_gain.reshape(G, per_group * P_SIZE)
    return normed.reshape(WINDOW_LENGTH, SSM_CHANNEL_COUNT * P_SIZE).astype(jnp.bfloat16)

def reference(query, key_new, value_new, ssm_input, ssm_gate, ssm_b, ssm_c, log_decay, key_cache, value_cache, init_state, skip_gain, norm_gain, cache_length, span_start):
    attn_output = attention_part(query, key_new, value_new, key_cache, value_cache, cache_length, span_start)
    ssm_output = ssm_part(ssm_input, ssm_gate, ssm_b, ssm_c, log_decay, init_state, skip_gain, norm_gain, span_start)
    return (attn_output, ssm_output)
```

```python
import jax
import jax.numpy as jnp
from jax import lax
from jax.experimental import pallas as pl
from jax.experimental.pallas import tpu as pltpu
from jax.sharding import PartitionSpec as P

Z = 16
LANES = 4
TP = 8
PLANE = LANES * TP
DH = 128
P_SIZE = 64
SPAN = 256
KEYS = 1024
ROWS = 1024
UNIT = 256
UP = 8
DOWN = 7
SCALE = 128.0 ** -0.5
LOW = -1e30
MESH = pl.DeviceIdType.MESH
F32 = jnp.float32
BF16 = jnp.bfloat16


def dot(a, b, ca, cb):
    return lax.dot_general(a, b, (((ca,), (cb,)), ((), ())), preferred_element_type=F32)


def kernel(
    length_ref, start_ref, q_ref, k_ref, v_ref, xw_ref, dec_ref, b_ref, c_ref,
    kc_ref, vc_ref, init_ref, gain_ref, x_ref, gate_ref,
    attn_ref, ssm_ref,
    a_send, a_recv, kv_send, kv_recv, g_recv, cache, fresh, states,
    cum_ref, y_ref, prior, o1, m1, l1, e_send, e_recv, s_send, s_recv,
    a_ss, a_rs, kv_ss, kv_rs, g_ss, g_rs,
    up_ss, up_rs, dn_ss, dn_rs, e_ss, e_rs, s_ss, s_rs,
):
    seq, tp = lax.axis_index("seq"), lax.axis_index("tp")
    z, lane = seq // LANES, lax.rem(seq, LANES)
    me = lane * TP + tp
    above = lax.rem(z + 1, Z) * LANES + lane
    below = lax.rem(z + Z - 1, Z) * LANES + lane

    def place(d):
        return (z * LANES + d // TP, lax.rem(d, TP))

    barrier = pltpu.get_barrier_semaphore()

    def greet(i, unused):
        pl.semaphore_signal(
            barrier, inc=1, device_id=place(lax.rem(me + i, PLANE)), device_id_type=MESH
        )
        return unused

    lax.fori_loop(1, PLANE, greet, 0)
    for other in (above, below):
        pl.semaphore_signal(barrier, inc=1, device_id=(other, tp), device_id_type=MESH)

    cache[z, 0:64, :] = kc_ref[...]
    cache[z, 64:128, :] = vc_ref[...]
    q = q_ref[...].astype(F32)
    xw = xw_ref[...].astype(F32)
    dec = dec_ref[...].astype(F32)
    bb = b_ref[...].astype(F32)
    cc = c_ref[...].astype(F32)
    kk = k_ref[...].astype(F32)
    vv = v_ref[...].astype(F32)

    def columns(a, first, count):
        return jnp.concatenate(
            [a[:, (first + j) * 128:(first + j + 1) * 128] for j in range(count)], 0
        ).astype(BF16)

    for t in range(TP):
        q_block = columns(q, t * 4, 4)
        bc_block = jnp.concatenate(
            [bb[:, t * 128:(t + 1) * 128], cc[:, t * 128:(t + 1) * 128]], 0
        ).astype(BF16)
        kv_send[t] = jnp.concatenate(
            [kk[:, t * 128:(t + 1) * 128], vv[:, t * 128:(t + 1) * 128]], 0
        ).astype(BF16)
        for l in range(LANES):
            d = l * TP + t
            a_send[d, 0:32, :] = q_block
            a_send[d, 32:48, :] = columns(xw, t * 8 + l * 2, 2)
            a_send[d, 48:64, :] = columns(dec, t * 8 + l * 2, 2)
            a_send[d, 64:80, :] = bc_block
    a_recv[me] = a_send[me]
    kv_recv[tp] = kv_send[tp]
    g_recv[tp] = gain_ref[...]
    pl.semaphore_wait(barrier, PLANE - 1 + 2)

    def up_copy(buf, ring, step):
        block = lax.rem(z + Z - step, Z)
        return pltpu.make_async_remote_copy(
            src_ref=buf.at[block], dst_ref=buf.at[block],
            send_sem=up_ss.at[ring, step], recv_sem=up_rs.at[ring, step],
            device_id=(above, tp), device_id_type=MESH,
        )

    def dn_copy(buf, ring, step):
        block = lax.rem(z + step, Z)
        return pltpu.make_async_remote_copy(
            src_ref=buf.at[block], dst_ref=buf.at[block],
            send_sem=dn_ss.at[ring, step], recv_sem=dn_rs.at[ring, step],
            device_id=(below, tp), device_id_type=MESH,
        )

    def up_wait(buf, ring, step):
        block = lax.rem(z + 2 * Z - 1 - step, Z)
        pltpu.make_async_remote_copy(
            src_ref=buf.at[block], dst_ref=buf.at[block],
            send_sem=up_ss.at[ring, step], recv_sem=up_rs.at[ring, step],
            device_id=(above, tp), device_id_type=MESH,
        ).wait_recv()

    def dn_wait(buf, ring, step):
        block = lax.rem(z + 1 + step, Z)
        pltpu.make_async_remote_copy(
            src_ref=buf.at[block], dst_ref=buf.at[block],
            send_sem=dn_ss.at[ring, step], recv_sem=dn_rs.at[ring, step],
            device_id=(below, tp), device_id_type=MESH,
        ).wait_recv()

    def first(buf, ring):
        up_copy(buf, ring, 0).start()
        dn_copy(buf, ring, 0).start()

    def tick(buf, ring, step):
        up_wait(buf, ring, step - 1)
        if step < UP:
            up_copy(buf, ring, step).start()
        if step <= DOWN:
            dn_wait(buf, ring, step - 1)
        if step < DOWN:
            dn_copy(buf, ring, step).start()

    def sent(buf, ring):
        for step in range(UP):
            up_copy(buf, ring, step).wait_send()
        for step in range(DOWN):
            dn_copy(buf, ring, step).wait_send()

    def kv_copy(t, slot):
        return pltpu.make_async_remote_copy(
            src_ref=kv_send.at[t], dst_ref=kv_recv.at[slot],
            send_sem=kv_ss.at[t], recv_sem=kv_rs.at[slot],
            device_id=(seq, t), device_id_type=MESH,
        )

    def g_copy(t, slot):
        return pltpu.make_async_remote_copy(
            src_ref=gain_ref, dst_ref=g_recv.at[slot],
            send_sem=g_ss.at[t], recv_sem=g_rs.at[slot],
            device_id=(seq, t), device_id_type=MESH,
        )

    def a_copy(d, slot):
        return pltpu.make_async_remote_copy(
            src_ref=a_send.at[d], dst_ref=a_recv.at[slot],
            send_sem=a_ss.at[d], recv_sem=a_rs.at[slot],
            device_id=place(d), device_id_type=MESH,
        )

    def e_copy(d, slot):
        return pltpu.make_async_remote_copy(
            src_ref=e_send.at[d], dst_ref=e_recv.at[slot],
            send_sem=e_ss.at[d], recv_sem=e_rs.at[slot],
            device_id=place(d), device_id_type=MESH,
        )

    def s_copy(d, slot):
        return pltpu.make_async_remote_copy(
            src_ref=s_send.at[d], dst_ref=s_recv.at[slot],
            send_sem=s_ss.at[d], recv_sem=s_rs.at[slot],
            device_id=place(d), device_id_type=MESH,
        )

    def over_plane(act):
        def body(i, unused):
            act(lax.rem(me + i, PLANE))
            return unused

        lax.fori_loop(1, PLANE, body, 0)

    def over_tp(act):
        def body(i, unused):
            act(lax.rem(tp + i, TP))
            return unused

        lax.fori_loop(1, TP, body, 0)

    first(cache, 0)
    over_tp(lambda t: kv_copy(t, tp).start())
    over_plane(lambda d: a_copy(d, me).start())
    over_tp(lambda t: g_copy(t, tp).start())

    prior[...] = jnp.transpose(
        init_ref[pl.ds(lane * 4, 4)].reshape(4 * P_SIZE, 128)
    )
    for step in range(1, 4):
        tick(cache, 0, step)

    over_tp(lambda t: kv_copy(t, t).wait_recv())
    kv = kv_recv[...].astype(F32)
    fresh[z, 0:64, :] = kv[:, 0:8, :].reshape(64, DH).astype(BF16)
    fresh[z, 64:128, :] = kv[:, 8:16, :].reshape(64, DH).astype(BF16)
    first(fresh, 1)
    tick(cache, 0, 4)
    over_plane(lambda d: a_copy(d, d).wait_recv())

    def halves(first_row):
        part = a_recv[:, first_row:first_row + 16, :].astype(F32)
        return part[:, 0:8, :].reshape(SPAN, 128), part[:, 8:16, :].reshape(SPAN, 128)

    b_all, c_all = halves(64)
    b_all, c_all = b_all.astype(BF16), c_all.astype(BF16)
    x_all = jnp.concatenate(halves(32), 1)
    d_all = jnp.concatenate(halves(48), 1).astype(BF16)
    row = lax.broadcasted_iota(jnp.int32, (SPAN, SPAN), 0)
    col = lax.broadcasted_iota(jnp.int32, (SPAN, SPAN), 1)
    lower = row >= col
    ones = lower.astype(F32).astype(BF16)
    cum = dot(ones, d_all, 1, 0)
    end = cum[SPAN - 1:SPAN, :]
    local = dot(b_all, (x_all * jnp.exp(end - cum)).astype(BF16), 0, 0)
    states[z, 0:128, :] = local.astype(BF16)
    high = end.astype(BF16).astype(F32)
    states[z, 128:144, :] = jnp.concatenate(
        [jnp.broadcast_to(high, (8, SPAN)), jnp.broadcast_to(end - high, (8, SPAN))], 0
    ).astype(BF16)
    first(states, 2)
    cum_ref[...] = cum

    x_all = x_all.astype(BF16)
    cum_t = dot(d_all, ones, 0, 1)
    pair = dot(c_all, b_all, 1, 1)
    first_half = lax.broadcasted_iota(jnp.int32, (SPAN, 128), 1) < P_SIZE
    for half in range(2):
        parts = []
        for j in (2 * half, 2 * half + 1):
            gap = cum[:, j * P_SIZE:j * P_SIZE + 1] - cum_t[j * P_SIZE:j * P_SIZE + 1, :]
            fade = jnp.where(lower, jnp.exp(jnp.where(lower, gap, 0.0)), 0.0)
            parts.append(
                dot((pair * fade).astype(BF16), x_all[:, half * 128:(half + 1) * 128], 1, 0)
            )
            tick(cache, 0, 5 + j)
            tick(fresh, 1, 1 + j)
            tick(states, 2, 1 + j)
        y_ref[:, half * 128:(half + 1) * 128] = jnp.where(first_half, parts[0], parts[1])

    key_at = lax.broadcasted_iota(jnp.int32, (1, KEYS), 1)
    key_place = (key_at // 64) * SPAN + lane * 64 + lax.rem(key_at, 64)
    row_at = lax.broadcasted_iota(jnp.int32, (UNIT, 1), 0)

    def part(u, buf, usable):
        queries = a_recv[pl.ds(u * 8, 8), 0:32, :].reshape(UNIT, DH)
        keys = buf[:, 0:64, :].reshape(KEYS, DH)
        values = buf[:, 64:128, :].reshape(KEYS, DH)
        scores = jnp.where(usable, dot(queries, keys, 1, 1) * SCALE, LOW)
        top = jnp.max(scores, axis=1, keepdims=True)
        weights = jnp.exp(scores - top)
        total = jnp.sum(weights, axis=1, keepdims=True)
        return top, total, dot(weights.astype(BF16), values, 1, 0)

    cached = key_place < length_ref[0]
    for u in range(ROWS // UNIT):
        top, total, mixed = part(u, cache, cached)
        m1[u * UNIT:(u + 1) * UNIT, :] = top
        l1[u * UNIT:(u + 1) * UNIT, :] = total
        o1[u * UNIT:(u + 1) * UNIT, :] = mixed
        tick(fresh, 1, 5 + u)
        tick(states, 2, 5 + u)

    def lap(k, unused):
        tail = states[k, 128:144, :].astype(F32)
        log = tail[0:1, :] + tail[8:9, :]
        prior[...] = prior[...] * jnp.exp(log) + states[k, 0:128, :].astype(F32)
        return unused

    lax.fori_loop(0, z, lap, 0)
    y = y_ref[...] + jnp.exp(cum_ref[...]) * dot(c_all, prior[...].astype(BF16), 1, 0)
    e_send[:, 32:48, :] = jnp.concatenate(
        [y[:, 0:128].reshape(PLANE, 8, 128), y[:, 128:256].reshape(PLANE, 8, 128)], 1
    ).astype(BF16)

    spot = (
        lax.broadcasted_iota(jnp.int32, (1, 32, 128), 1)
        == lax.broadcasted_iota(jnp.int32, (1, 32, 128), 2)
    ).astype(F32)
    for u in range(ROWS // UNIT):
        query_place = z * SPAN + u * 64 + (row_at // 32) * 8 + lax.rem(row_at, 8)
        usable = (key_place >= start_ref[0]) & (key_place <= query_place)
        top, total, mixed = part(u, fresh, usable)
        top1, total1 = m1[u * UNIT:(u + 1) * UNIT, :], l1[u * UNIT:(u + 1) * UNIT, :]
        both = jnp.maximum(top, top1)
        by, by1 = jnp.exp(top - both), jnp.exp(top1 - both)
        total = total * by + total1 * by1
        mixed = (mixed * by + o1[u * UNIT:(u + 1) * UNIT, :] * by1) / total
        e_send[u * 8:(u + 1) * 8, 0:32, :] = mixed.astype(BF16).reshape(8, 32, DH)
        size = jnp.broadcast_to(both + jnp.log(total), (UNIT, 128)).reshape(8, 32, 128)
        s_send[u * 8:(u + 1) * 8] = jnp.broadcast_to(
            jnp.sum(size * spot, axis=1, keepdims=True), (8, 8, 128)
        )

    e_recv[me] = e_send[me]
    s_recv[me] = s_send[me]
    over_plane(lambda d: s_copy(d, me).start())
    over_plane(lambda d: e_copy(d, me).start())
    over_tp(lambda t: g_copy(t, t).wait_recv())
    over_plane(lambda d: s_copy(d, d).wait_recv())
    over_plane(lambda d: e_copy(d, d).wait_recv())

    for t in range(TP):
        sizes = [
            jnp.sum(s_recv[l * TP + t, 0:1, :] * spot[0], axis=1, keepdims=True)
            for l in range(LANES)
        ]
        most = jnp.maximum(jnp.maximum(sizes[0], sizes[1]), jnp.maximum(sizes[2], sizes[3]))
        shares = [jnp.exp(size - most) for size in sizes]
        whole = shares[0] + shares[1] + shares[2] + shares[3]
        out = sum(
            share * e_recv[l * TP + t, 0:32, :].astype(F32) for l, share in enumerate(shares)
        ) / whole
        for h in range(4):
            at = (t * 4 + h) * 128
            attn_ref[:, at:at + 128] = out[h * 8:(h + 1) * 8, :].astype(BF16)

        gated, squares = [], 0.0
        for l in range(LANES):
            y_part = e_recv[l * TP + t, 32:48, :].astype(F32)
            for half in range(2):
                r = l * 2 + half
                at = t * 1024 + r * 128
                gate = gate_ref[:, at:at + 128].astype(F32)
                value = y_part[half * 8:(half + 1) * 8, :] + g_recv[
                    t, 8 + r:9 + r, :
                ] * x_ref[:, at:at + 128].astype(F32)
                value = value * (gate / (1.0 + jnp.exp(-gate)))
                squares = squares + value * value
                gated.append(value)
        scale = lax.rsqrt(jnp.sum(squares, axis=1, keepdims=True) * (1.0 / 1024) + 1e-5)
        for r in range(8):
            at = t * 1024 + r * 128
            ssm_ref[:, at:at + 128] = (gated[r] * scale * g_recv[t, r:r + 1, :]).astype(BF16)

    over_tp(lambda t: kv_copy(t, tp).wait_send())
    over_tp(lambda t: g_copy(t, tp).wait_send())
    over_plane(lambda d: a_copy(d, me).wait_send())
    over_plane(lambda d: s_copy(d, me).wait_send())
    over_plane(lambda d: e_copy(d, me).wait_send())
    sent(cache, 0)
    sent(fresh, 1)
    sent(states, 2)


def local(
    query, key_new, value_new, ssm_input, ssm_gate, ssm_b, ssm_c, log_decay,
    key_cache, value_cache, init_state, skip_gain, norm_gain, cache_length, span_start,
):
    token = (lax.axis_index("seq") * TP + lax.axis_index("tp")) * 8 + jnp.arange(8)
    decay = jnp.where(token[:, None] >= span_start[0], log_decay.astype(F32), 0.0)
    in_weight = jnp.sqrt(-jnp.expm1(2.0 * decay))
    weighted = (
        (ssm_input.reshape(8, 128, P_SIZE).astype(F32) * in_weight[:, :, None])
        .reshape(8, 8192)
        .astype(BF16)
    )
    spread = jnp.repeat(decay.astype(BF16), P_SIZE, axis=1)
    gains = jnp.concatenate(
        [norm_gain.reshape(8, 128), jnp.repeat(skip_gain, P_SIZE).reshape(8, 128)], 0
    )
    vmem = pl.BlockSpec(memory_space=pltpu.VMEM)
    smem = pl.BlockSpec(memory_space=pltpu.SMEM)
    dma = pltpu.SemaphoreType.DMA
    return pl.pallas_call(
        kernel,
        out_shape=(
            jax.ShapeDtypeStruct((8, 4096), BF16),
            jax.ShapeDtypeStruct((8, 8192), BF16),
        ),
        in_specs=[smem] * 2 + [vmem] * 13,
        out_specs=(vmem, vmem),
        scratch_shapes=[
            pltpu.VMEM((PLANE, 80, 128), BF16),
            pltpu.VMEM((PLANE, 80, 128), BF16),
            pltpu.VMEM((TP, 16, 128), BF16),
            pltpu.VMEM((TP, 16, 128), BF16),
            pltpu.VMEM((TP, 16, 128), F32),
            pltpu.VMEM((Z, 128, DH), BF16),
            pltpu.VMEM((Z, 128, DH), BF16),
            pltpu.VMEM((Z, 144, SPAN), BF16),
            pltpu.VMEM((SPAN, SPAN), F32),
            pltpu.VMEM((SPAN, SPAN), F32),
            pltpu.VMEM((128, SPAN), F32),
            pltpu.VMEM((ROWS, DH), F32),
            pltpu.VMEM((ROWS, 1), F32),
            pltpu.VMEM((ROWS, 1), F32),
            pltpu.VMEM((PLANE, 48, 128), BF16),
            pltpu.VMEM((PLANE, 48, 128), BF16),
            pltpu.VMEM((PLANE, 8, 128), F32),
            pltpu.VMEM((PLANE, 8, 128), F32),
            dma((PLANE,)), dma((PLANE,)),
            dma((TP,)), dma((TP,)),
            dma((TP,)), dma((TP,)),
            dma((3, UP)), dma((3, UP)),
            dma((3, DOWN)), dma((3, DOWN)),
            dma((PLANE,)), dma((PLANE,)),
            dma((PLANE,)), dma((PLANE,)),
        ],
        compiler_params=pltpu.CompilerParams(
            collective_id=0, has_side_effects=True, vmem_limit_bytes=40 * 1024 * 1024
        ),
        name="mixers",
    )(
        cache_length, span_start, query, key_new, value_new, weighted, spread, ssm_b, ssm_c,
        key_cache, value_cache, init_state, gains, ssm_input, ssm_gate,
    )


def solution(mesh):
    rows = P(("seq", "tp"), None)
    placed = (rows,) * 8 + (
        P("seq", "tp"),
        P("seq", "tp"),
        P("tp", None, None),
        P("tp"),
        P("tp"),
        P(),
        P(),
    )
    return jax.shard_map(
        local, mesh=mesh, in_specs=placed, out_specs=(rows, rows), check_vma=False
    )
```

```python
import jax
import jax.numpy as jnp
from jax import lax
from jax.experimental import pallas as pl
from jax.experimental.pallas import tpu as pltpu
from jax.sharding import PartitionSpec as P

Z = 16
LANES = 4
TP = 8
PLANE = LANES * TP
DH = 128
P_SIZE = 64
SPAN = 256
KEYS = 1024
ROWS = 1024
UNIT = 256
REACH = 4
SCALE = 128.0 ** -0.5
LOW = -1e30
MESH = pl.DeviceIdType.MESH
F32 = jnp.float32
BF16 = jnp.bfloat16


def dot(a, b, ca, cb):
    return lax.dot_general(a, b, (((ca,), (cb,)), ((), ())), preferred_element_type=F32)


def in_weights(decay):
    u = 2.0 * decay
    series = 1.0 + u * (1.0 / 12)
    for k in range(11, 1, -1):
        series = 1.0 + u * (1.0 / k) * series
    return jnp.sqrt(jnp.where(u < -1.0, 1.0 - jnp.exp(u), -u * series))


def kernel(
    length_ref, start_ref, skip_ref,
    q_hbm, k_hbm, v_hbm, x_hbm, dec_hbm, b_hbm, c_hbm, kc_hbm, vc_hbm, init_hbm, norm_hbm, gate_hbm,
    attn_ref, ssm_ref,
    q_ref, k_ref, v_ref, x_ref, dec_ref, b_ref, c_ref, kc_ref, vc_ref, init_ref, gain_ref, gate_ref,
    a_send, a_recv, q_send, q_recv, kv_send, kv_recv, g_recv, cache, fresh,
    p1_send, p1_recv, p2_send, p2_recv, p3_send, p3_recv,
    cum_ref, y_ref, o1, m1, l1, o_send, o_recv, y_send, y_recv,
    in_sem, a_ss, a_rs, q_ss, q_rs, kv_ss, kv_rs, g_ss, g_rs, z_ss, z_rs,
    p1_ss, p1_rs, p2_ss, p2_rs, p3_ss, p3_rs, o_ss, o_rs, y_ss, y_rs,
):
    seq, tp = lax.axis_index("seq"), lax.axis_index("tp")
    z, lane = seq // LANES, lax.rem(seq, LANES)
    me = lane * TP + tp
    four, member = z // 4, lax.rem(z, 4)

    loads = [
        pltpu.make_async_copy(src, dst, in_sem.at[n])
        for n, (src, dst) in enumerate(
            (
                (x_hbm, x_ref), (b_hbm, b_ref), (c_hbm, c_ref), (dec_hbm, dec_ref),
                (k_hbm, k_ref), (v_hbm, v_ref), (kc_hbm, kc_ref), (vc_hbm, vc_ref),
                (q_hbm, q_ref), (norm_hbm, gain_ref.at[pl.ds(0, 8)]),
                (init_hbm.at[lane * 4 + member], init_ref), (gate_hbm, gate_ref),
            )
        )
    ]
    for load in loads:
        load.start()
    fresh[...] = jnp.zeros_like(fresh)

    def place(d):
        return (z * LANES + d // TP, lax.rem(d, TP))

    def along(k):
        return (lax.rem(z + Z + k, Z) * LANES + lane, tp)

    barrier = pltpu.get_barrier_semaphore()

    def greet(i, unused):
        pl.semaphore_signal(
            barrier, inc=1, device_id=place(lax.rem(me + i, PLANE)), device_id_type=MESH
        )
        return unused

    offsets = [k for k in range(-REACH, REACH + 1) if k] + [8]
    for k in offsets:
        pl.semaphore_signal(barrier, inc=1, device_id=along(k), device_id_type=MESH)
    lax.fori_loop(1, PLANE, greet, 0)

    for load in loads[:8]:
        load.wait()
    cache[z, 0:64, :] = kc_ref[...]
    cache[z, 64:128, :] = vc_ref[...]
    xx = x_ref[...].astype(F32)
    dec = dec_ref[...].astype(F32)
    bb = b_ref[...].astype(F32)
    cc = c_ref[...].astype(F32)
    kk = k_ref[...].astype(F32)
    vv = v_ref[...].astype(F32)

    def columns(a, first, count):
        return jnp.concatenate(
            [a[:, (first + j) * 128:(first + j + 1) * 128] for j in range(count)], 0
        ).astype(BF16)

    dec_block = jnp.concatenate([dec, dec], 0).astype(BF16)
    for t in range(TP):
        at = slice(t * 128, (t + 1) * 128)
        bc_block = jnp.concatenate([bb[:, at], cc[:, at]], 0).astype(BF16)
        kv_send[t] = jnp.concatenate([kk[:, at], vv[:, at]], 0).astype(BF16)
        for l in range(LANES):
            d = l * TP + t
            a_send[d, 0:16, :] = columns(xx, t * 8 + l * 2, 2)
            a_send[d, 16:32, :] = bc_block
            a_send[d, 32:48, :] = dec_block
    a_recv[me] = a_send[me]
    kv_recv[tp] = kv_send[tp]
    for load in loads[8:10]:
        load.wait()
    qq = q_ref[...].astype(F32)
    for t in range(TP):
        q_send[t] = columns(qq, t * 4, 4)
    q_recv[me] = q_send[tp]
    tile_row = lax.broadcasted_iota(jnp.int32, (8, 128), 0)
    tile_lane = lax.broadcasted_iota(jnp.int32, (8, 128), 1)
    skips = jnp.zeros((8, 128), F32)
    for h in range(16):
        skips = jnp.where(tile_row * 2 + tile_lane // P_SIZE == h, skip_ref[h], skips)
    gain_ref[8:16, :] = skips
    g_recv[tp] = gain_ref[...]
    pl.semaphore_wait(barrier, PLANE - 1 + len(offsets))

    def copy(src, dst, send, recv, device):
        return pltpu.make_async_remote_copy(
            src_ref=src, dst_ref=dst, send_sem=send, recv_sem=recv,
            device_id=device, device_id_type=MESH,
        )

    def kv_copy(t, slot):
        return copy(kv_send.at[t], kv_recv.at[slot], kv_ss.at[t], kv_rs.at[slot], (seq, t))

    def g_copy(t, slot):
        return copy(gain_ref, g_recv.at[slot], g_ss.at[t], g_rs.at[slot], (seq, t))

    def a_copy(d, slot):
        return copy(a_send.at[d], a_recv.at[slot], a_ss.at[d], a_rs.at[slot], place(d))

    def q_copy(d, slot):
        return copy(
            q_send.at[lax.rem(d, TP)], q_recv.at[slot], q_ss.at[d], q_rs.at[slot], place(d)
        )

    def o_copy(d, slot):
        return copy(o_send.at[d], o_recv.at[slot], o_ss.at[d], o_rs.at[slot], place(d))

    def y_copy(d, slot):
        return copy(y_send.at[d], y_recv.at[slot], y_ss.at[d], y_rs.at[slot], place(d))

    def over_plane(act):
        def body(i, unused):
            act(lax.rem(me + i, PLANE))
            return unused

        lax.fori_loop(1, PLANE, body, 0)

    def over_tp(act):
        def body(i, unused):
            act(lax.rem(tp + i, TP))
            return unused

        lax.fori_loop(1, TP, body, 0)

    def hop(buf, ring, from_block, k, mark):
        block = lax.rem(z + Z + from_block, Z)
        return copy(
            buf.at[block], buf.at[block], z_ss.at[ring, mark], z_rs.at[ring, block], along(k)
        )

    def landed(buf, ring, k):
        hop(buf, ring, k, 1, 0).wait_recv()

    def wrapped(k):
        return lax.rem(z + Z + k, Z)

    near = [(0, k, 4 + k, wrapped(k) > z) for k in (4, 3, -3, 2, -2, 1, -1)]
    near.insert(1, (0, -4, 0, z <= 6))
    up_on = [(-4, k, 8 + k, (z >= 4) & (z + k < Z)) for k in (4, 3, 2, 1)]
    down_on = [(4, -k, 12 + k, wrapped(4) <= 3 + k) for k in (3, 2, 1)]
    hops = near + up_on + down_on

    def launch(buf, ring, which, causal):
        for from_block, k, mark, needed in which:
            if causal:
                pl.when(needed)(lambda f=from_block, k=k, m=mark: hop(buf, ring, f, k, m).start())
            else:
                hop(buf, ring, from_block, k, mark).start()

    def arrive(buf, ring, k, causal, also=None):
        if causal:
            needed = wrapped(k) < z
            if also is not None:
                needed = needed | also
            pl.when(needed)(lambda: landed(buf, ring, k))
        else:
            landed(buf, ring, k)

    def sent(buf, ring, causal):
        for from_block, k, mark, needed in hops:
            if causal:
                pl.when(needed)(
                    lambda f=from_block, k=k, m=mark: hop(buf, ring, f, k, m).wait_send()
                )
            else:
                hop(buf, ring, from_block, k, mark).wait_send()

    others = (-1, 1, -2, 2, -3, 3, -5, 5, -6, 6, -7, 7, 8)

    over_tp(lambda t: kv_copy(t, tp).start())
    over_plane(lambda d: a_copy(d, me).start())
    launch(cache, 0, near, False)
    over_plane(lambda d: q_copy(d, me).start())
    over_tp(lambda t: g_copy(t, tp).start())

    arrive(cache, 0, -4, False)
    launch(cache, 0, up_on, False)
    arrive(cache, 0, 4, False)
    launch(cache, 0, down_on, False)

    over_tp(lambda t: kv_copy(t, t).wait_recv())
    kv = kv_recv[...].astype(F32)
    fresh[z, 0:64, :] = kv[:, 0:8, :].reshape(64, DH).astype(BF16)
    fresh[z, 64:128, :] = kv[:, 8:16, :].reshape(64, DH).astype(BF16)
    launch(fresh, 1, near, True)
    over_plane(lambda d: a_copy(d, d).wait_recv())

    def halves(first_row):
        part = a_recv[:, first_row:first_row + 16, :].astype(F32)
        return part[:, 0:8, :].reshape(SPAN, 128), part[:, 8:16, :].reshape(SPAN, 128)

    row = lax.broadcasted_iota(jnp.int32, (SPAN, SPAN), 0)
    col = lax.broadcasted_iota(jnp.int32, (SPAN, SPAN), 1)
    lower = row >= col
    ones = lower.astype(F32).astype(BF16)
    b_all, c_all = halves(16)
    b_all, c_all = b_all.astype(BF16), c_all.astype(BF16)
    mine = (
        lax.broadcasted_iota(jnp.int32, (128, SPAN), 0)
        == tp * 16 + lane * 4 + lax.broadcasted_iota(jnp.int32, (128, SPAN), 1) // P_SIZE
    )
    decay = dot(halves(32)[0].astype(BF16), mine.astype(F32).astype(BF16), 1, 0)
    decay = jnp.where(z * SPAN + row >= start_ref[0], decay, 0.0)
    d_all = decay.astype(BF16)
    x_all = jnp.concatenate(halves(0), 1) * in_weights(decay)
    cum = dot(ones, d_all, 1, 0)
    end = cum[SPAN - 1:SPAN, :]
    local = dot((x_all * jnp.exp(end - cum)).astype(BF16), b_all, 0, 0).astype(BF16)

    def log_rows(log):
        high = log.astype(BF16).astype(F32)
        return jnp.concatenate(
            [jnp.broadcast_to(high, (8, 128)), jnp.broadcast_to(log - high, (8, 128))], 0
        ).astype(BF16)

    for h in range(4):
        p1_send[h, 0:64, :] = local[h * P_SIZE:(h + 1) * P_SIZE, :]
        p1_send[h, 64:80, :] = log_rows(
            jnp.broadcast_to(end[:, h * P_SIZE:h * P_SIZE + 1], (1, 128))
        )
    p1_recv[member] = p1_send[member]

    def peer(k):
        return lax.rem(member + k, 4)

    def in_four(m):
        return ((four * 4 + m) * LANES + lane, tp)

    def p1_copy(m, slot):
        return copy(p1_send.at[m], p1_recv.at[slot], p1_ss.at[m], p1_rs.at[slot], in_four(m))

    def p2_copy(f, slot):
        return copy(
            p2_send, p2_recv.at[slot], p2_ss.at[f], p2_rs.at[slot],
            ((f * 4 + member) * LANES + lane, tp),
        )

    def p3_copy(m, slot):
        return copy(p3_send.at[m], p3_recv.at[slot], p3_ss.at[m], p3_rs.at[slot], in_four(m))

    for k in (1, 2, 3):
        p1_copy(peer(k), member).start()
    cum_ref[...] = cum

    x_all = x_all.astype(BF16)
    cum_t = dot(d_all, ones, 0, 1)
    pair = dot(c_all, b_all, 1, 1)
    first_half = lax.broadcasted_iota(jnp.int32, (SPAN, 128), 1) < P_SIZE
    for half in range(2):
        parts = []
        for j in (2 * half, 2 * half + 1):
            gap = cum[:, j * P_SIZE:j * P_SIZE + 1] - cum_t[j * P_SIZE:j * P_SIZE + 1, :]
            fade = jnp.where(lower, jnp.exp(jnp.where(lower, gap, 0.0)), 0.0)
            parts.append(
                dot((pair * fade).astype(BF16), x_all[:, half * 128:(half + 1) * 128], 1, 0)
            )
        y_ref[:, half * 128:(half + 1) * 128] = jnp.where(first_half, parts[0], parts[1])

    arrive(fresh, 1, -4, True)
    launch(fresh, 1, up_on, True)
    arrive(fresh, 1, 4, True, wrapped(4) <= 6)
    launch(fresh, 1, down_on, True)

    for k in (1, 2, 3):
        p1_copy(peer(k), peer(k)).wait_recv()

    def state_of(tile):
        tail = tile[64:80, :].astype(F32)
        return tile[0:64, :].astype(F32), tail[0:1, :] + tail[8:9, :]

    steps = [state_of(p1_recv[m]) for m in range(4)]
    total, total_log = steps[0]
    for add, log in steps[1:]:
        total, total_log = total * jnp.exp(log) + add, total_log + log
    p2_send[0:64, :] = total.astype(BF16)
    p2_send[64:80, :] = log_rows(total_log)
    for k in (1, 2, 3):
        pl.when(four + k < 4)(lambda k=k: p2_copy(four + k, four).start())

    key_at = lax.broadcasted_iota(jnp.int32, (1, KEYS), 1)
    key_place = (key_at // 64) * SPAN + lane * 64 + lax.rem(key_at, 64)
    row_at = lax.broadcasted_iota(jnp.int32, (UNIT, 1), 0)

    def part(u, buf, usable):
        queries = q_recv[pl.ds(u * 8, 8)].reshape(UNIT, DH)
        keys = buf[:, 0:64, :].reshape(KEYS, DH)
        values = buf[:, 64:128, :].reshape(KEYS, DH)
        scores = jnp.where(usable, dot(queries, keys, 1, 1) * SCALE, LOW)
        top = jnp.max(scores, axis=1, keepdims=True)
        weights = jnp.exp(scores - top)
        total = jnp.sum(weights, axis=1, keepdims=True)
        return top, total, dot(weights.astype(BF16), values, 1, 0)

    over_plane(lambda d: q_copy(d, d).wait_recv())
    for k in others:
        arrive(cache, 0, k, False)
    cached = key_place < length_ref[0]
    for u in range(ROWS // UNIT):
        top, weight, mixed = part(u, cache, cached)
        m1[u * UNIT:(u + 1) * UNIT, :] = top
        l1[u * UNIT:(u + 1) * UNIT, :] = weight
        o1[u * UNIT:(u + 1) * UNIT, :] = mixed

    loads[10].wait()
    for k in (1, 2, 3):
        pl.when(four - k >= 0)(lambda k=k: p2_copy(four, four - k).wait_recv())

    def lap(f, prior):
        add, log = state_of(p2_recv[f])
        return prior * jnp.exp(log) + add

    prior = lax.fori_loop(0, four, lap, init_ref[...])
    for m in range(4):
        p3_send[m] = prior.astype(BF16)
        if m < 3:
            prior = prior * jnp.exp(steps[m][1]) + steps[m][0]
    p3_recv[member] = p3_send[member]
    for k in (1, 2, 3):
        p3_copy(peer(k), member).start()

    for k in others:
        arrive(fresh, 1, k, True)
    spot = (
        lax.broadcasted_iota(jnp.int32, (1, 32, 128), 1)
        == lax.broadcasted_iota(jnp.int32, (1, 32, 128), 2)
    ).astype(F32)
    spot_row = lax.broadcasted_iota(jnp.int32, (8, 16, 128), 1)
    for u in range(ROWS // UNIT):
        query_place = z * SPAN + u * 64 + (row_at // 32) * 8 + lax.rem(row_at, 8)
        usable = (key_place >= start_ref[0]) & (key_place <= query_place)
        top, weight, mixed = part(u, fresh, usable)
        top1, weight1 = m1[u * UNIT:(u + 1) * UNIT, :], l1[u * UNIT:(u + 1) * UNIT, :]
        both = jnp.maximum(top, top1)
        by, by1 = jnp.exp(top - both), jnp.exp(top1 - both)
        weight = weight * by + weight1 * by1
        mixed = (mixed * by + o1[u * UNIT:(u + 1) * UNIT, :] * by1) / weight
        o_send[u * 8:(u + 1) * 8, 0:32, :] = mixed.astype(BF16).reshape(8, 32, DH)
        size = jnp.broadcast_to(both + jnp.log(weight), (UNIT, 128)).reshape(8, 32, 128)
        size = jnp.sum(size * spot, axis=1, keepdims=True)
        high = size.astype(BF16).astype(F32)
        middle = (size - high).astype(BF16).astype(F32)
        o_send[u * 8:(u + 1) * 8, 32:48, :] = jnp.where(
            spot_row < 8, high, jnp.where(spot_row < 15, middle, size - high - middle)
        ).astype(BF16)
    o_recv[me] = o_send[me]
    over_plane(lambda d: o_copy(d, me).start())

    for k in (1, 2, 3):
        p3_copy(peer(k), peer(k)).wait_recv()
    incoming = p3_recv[...].reshape(SPAN, 128)
    y = y_ref[...] + jnp.exp(cum_ref[...]) * dot(c_all, incoming, 1, 1)
    y_send[...] = jnp.concatenate(
        [y[:, 0:128].reshape(PLANE, 8, 128), y[:, 128:256].reshape(PLANE, 8, 128)], 1
    ).astype(BF16)
    y_recv[me] = y_send[me]
    over_plane(lambda d: y_copy(d, me).start())

    over_plane(lambda d: o_copy(d, d).wait_recv())
    for t in range(TP):
        sizes = []
        for l in range(LANES):
            tile = o_recv[l * TP + t, 32:48, :].astype(F32)
            line = tile[0:1, :] + tile[8:9, :] + tile[15:16, :]
            sizes.append(jnp.sum(line * spot[0], axis=1, keepdims=True))
        most = jnp.maximum(jnp.maximum(sizes[0], sizes[1]), jnp.maximum(sizes[2], sizes[3]))
        shares = [jnp.exp(size - most) for size in sizes]
        whole = shares[0] + shares[1] + shares[2] + shares[3]
        out = sum(
            share * o_recv[l * TP + t, 0:32, :].astype(F32) for l, share in enumerate(shares)
        ) / whole
        for h in range(4):
            at = (t * 4 + h) * 128
            attn_ref[:, at:at + 128] = out[h * 8:(h + 1) * 8, :].astype(BF16)

    over_tp(lambda t: g_copy(t, t).wait_recv())
    loads[11].wait()
    over_plane(lambda d: y_copy(d, d).wait_recv())
    for t in range(TP):
        gated, squares = [], 0.0
        for l in range(LANES):
            y_part = y_recv[l * TP + t].astype(F32)
            for half in range(2):
                r = l * 2 + half
                at = t * 1024 + r * 128
                gate = gate_ref[:, at:at + 128].astype(F32)
                value = y_part[half * 8:(half + 1) * 8, :] + g_recv[
                    t, 8 + r:9 + r, :
                ] * x_ref[:, at:at + 128].astype(F32)
                value = value * (gate / (1.0 + jnp.exp(-gate)))
                squares = squares + value * value
                gated.append(value)
        scale = lax.rsqrt(jnp.sum(squares, axis=1, keepdims=True) * (1.0 / 1024) + 1e-5)
        for r in range(8):
            at = t * 1024 + r * 128
            ssm_ref[:, at:at + 128] = (gated[r] * scale * g_recv[t, r:r + 1, :]).astype(BF16)

    over_tp(lambda t: kv_copy(t, tp).wait_send())
    over_tp(lambda t: g_copy(t, tp).wait_send())
    over_plane(lambda d: a_copy(d, me).wait_send())
    over_plane(lambda d: q_copy(d, me).wait_send())
    over_plane(lambda d: o_copy(d, me).wait_send())
    over_plane(lambda d: y_copy(d, me).wait_send())
    sent(cache, 0, False)
    sent(fresh, 1, True)
    for k in (1, 2, 3):
        p1_copy(peer(k), member).wait_send()
        pl.when(four + k < 4)(lambda k=k: p2_copy(four + k, four).wait_send())
        p3_copy(peer(k), member).wait_send()


def local(
    query, key_new, value_new, ssm_input, ssm_gate, ssm_b, ssm_c, log_decay,
    key_cache, value_cache, init_state, skip_gain, norm_gain, cache_length, span_start,
):
    vmem = pl.BlockSpec(memory_space=pltpu.VMEM)
    smem = pl.BlockSpec(memory_space=pltpu.SMEM)
    hbm = pl.BlockSpec(memory_space=pltpu.HBM)
    dma = pltpu.SemaphoreType.DMA
    return pl.pallas_call(
        kernel,
        out_shape=(
            jax.ShapeDtypeStruct((8, 4096), BF16),
            jax.ShapeDtypeStruct((8, 8192), BF16),
        ),
        in_specs=[smem] * 3 + [hbm] * 12,
        out_specs=(vmem, vmem),
        scratch_shapes=[
            pltpu.VMEM((8, 4096), BF16),
            pltpu.VMEM((8, 1024), BF16),
            pltpu.VMEM((8, 1024), BF16),
            pltpu.VMEM((8, 8192), BF16),
            pltpu.VMEM((8, 128), BF16),
            pltpu.VMEM((8, 1024), BF16),
            pltpu.VMEM((8, 1024), BF16),
            pltpu.VMEM((64, 128), BF16),
            pltpu.VMEM((64, 128), BF16),
            pltpu.VMEM((64, 128), F32),
            pltpu.VMEM((16, 128), F32),
            pltpu.VMEM((8, 8192), BF16),
            pltpu.VMEM((PLANE, 48, 128), BF16),
            pltpu.VMEM((PLANE, 48, 128), BF16),
            pltpu.VMEM((TP, 32, 128), BF16),
            pltpu.VMEM((PLANE, 32, 128), BF16),
            pltpu.VMEM((TP, 16, 128), BF16),
            pltpu.VMEM((TP, 16, 128), BF16),
            pltpu.VMEM((TP, 16, 128), F32),
            pltpu.VMEM((Z, 128, DH), BF16),
            pltpu.VMEM((Z, 128, DH), BF16),
            pltpu.VMEM((4, 80, 128), BF16),
            pltpu.VMEM((4, 80, 128), BF16),
            pltpu.VMEM((80, 128), BF16),
            pltpu.VMEM((4, 80, 128), BF16),
            pltpu.VMEM((4, 64, 128), BF16),
            pltpu.VMEM((4, 64, 128), BF16),
            pltpu.VMEM((SPAN, SPAN), F32),
            pltpu.VMEM((SPAN, SPAN), F32),
            pltpu.VMEM((ROWS, DH), F32),
            pltpu.VMEM((ROWS, 1), F32),
            pltpu.VMEM((ROWS, 1), F32),
            pltpu.VMEM((PLANE, 48, 128), BF16),
            pltpu.VMEM((PLANE, 48, 128), BF16),
            pltpu.VMEM((PLANE, 16, 128), BF16),
            pltpu.VMEM((PLANE, 16, 128), BF16),
            dma((12,)),
            dma((PLANE,)), dma((PLANE,)),
            dma((PLANE,)), dma((PLANE,)),
            dma((TP,)), dma((TP,)),
            dma((TP,)), dma((TP,)),
            dma((2, 16)), dma((2, Z)),
            dma((4,)), dma((4,)),
            dma((4,)), dma((4,)),
            dma((4,)), dma((4,)),
            dma((PLANE,)), dma((PLANE,)),
            dma((PLANE,)), dma((PLANE,)),
        ],
        compiler_params=pltpu.CompilerParams(
            collective_id=0, has_side_effects=True, vmem_limit_bytes=56 * 1024 * 1024
        ),
        name="mixers",
    )(
        cache_length, span_start, skip_gain,
        query, key_new, value_new, ssm_input, log_decay, ssm_b, ssm_c,
        key_cache, value_cache, init_state, norm_gain.reshape(8, 128), ssm_gate,
    )


def solution(mesh):
    rows = P(("seq", "tp"), None)
    placed = (rows,) * 8 + (
        P("seq", "tp"),
        P("seq", "tp"),
        P("tp", None, None),
        P("tp"),
        P("tp"),
        P(),
        P(),
    )
    return jax.shard_map(
        local, mesh=mesh, in_specs=placed, out_specs=(rows, rows), check_vma=False
    )
```

```python
import jax
import jax.numpy as jnp
from jax import lax
from jax.experimental import pallas as pl
from jax.experimental.pallas import tpu as pltpu
from jax.sharding import PartitionSpec as P

Z = 16
LANES = 4
TP = 8
PLANE = LANES * TP
DH = 128
P_SIZE = 64
SPAN = 256
KEYS = 1024
ROWS = 1024
UNIT = 256
REACH = 4
ROUNDS = 4
SCALE = 128.0 ** -0.5
LOW = -1e30
MESH = pl.DeviceIdType.MESH
F32 = jnp.float32
BF16 = jnp.bfloat16


def dot(a, b, ca, cb):
    return lax.dot_general(a, b, (((ca,), (cb,)), ((), ())), preferred_element_type=F32)


def in_weights(decay):
    u = 2.0 * decay
    series = 1.0 + u * (1.0 / 12)
    for k in range(11, 1, -1):
        series = 1.0 + u * (1.0 / k) * series
    return jnp.sqrt(jnp.where(u < -1.0, 1.0 - jnp.exp(u), -u * series))


def kernel(
    length_ref, start_ref, skip_ref,
    q_hbm, k_hbm, v_hbm, x_hbm, dec_hbm, b_hbm, c_hbm, kc_hbm, vc_hbm, init_hbm, norm_hbm, gate_hbm,
    attn_ref, ssm_ref,
    q_ref, k_ref, v_ref, x_ref, dec_ref, b_ref, c_ref, kc_ref, vc_ref, init_ref, gain_ref, gate_ref,
    a_send, a_recv, q_send, q_recv, kv_send, kv_recv, g_recv, cache, fresh,
    p1_send, p1_recv, p2_send, p2_recv, p3_send, p3_recv,
    cum_ref, y_ref, o1, m1, l1, o_send, o_recv, y_send, y_recv,
    in_sem, a_sem, q_sem, kv_sem, g_sem, z_ss, z_rs, p1_sem, p2_ss, p2_rs, p3_sem, o_sem, y_sem,
):
    seq, tp = lax.axis_index("seq"), lax.axis_index("tp")
    z, lane = seq // LANES, lax.rem(seq, LANES)
    me = lane * TP + tp
    four, member = z // 4, lax.rem(z, 4)

    loads = [
        pltpu.make_async_copy(src, dst, in_sem.at[n])
        for n, (src, dst) in enumerate(
            (
                (x_hbm, x_ref), (b_hbm, b_ref), (c_hbm, c_ref), (dec_hbm, dec_ref),
                (k_hbm, k_ref), (v_hbm, v_ref), (kc_hbm, kc_ref), (vc_hbm, vc_ref),
                (q_hbm, q_ref), (norm_hbm, gain_ref.at[pl.ds(0, 8)]),
                (init_hbm.at[lane * 4 + member], init_ref), (gate_hbm, gate_ref),
            )
        )
    ]
    for load in loads:
        load.start()
    fresh[...] = jnp.zeros_like(fresh)

    def place(d):
        return (z * LANES + d // TP, lax.rem(d, TP))

    def along(k):
        return (lax.rem(z + Z + k, Z) * LANES + lane, tp)

    barrier = pltpu.get_barrier_semaphore()

    def greet(i, unused):
        pl.semaphore_signal(
            barrier, inc=1, device_id=place(lax.rem(me + i, PLANE)), device_id_type=MESH
        )
        return unused

    offsets = [k for k in range(-REACH, REACH + 1) if k] + [8]
    for k in offsets:
        pl.semaphore_signal(barrier, inc=1, device_id=along(k), device_id_type=MESH)
    lax.fori_loop(1, PLANE, greet, 0)

    for load in loads[:8]:
        load.wait()
    cache[z, 0:64, :] = kc_ref[...]
    cache[z, 64:128, :] = vc_ref[...]
    xx = x_ref[...].astype(F32)
    dec = dec_ref[...].astype(F32)
    bb = b_ref[...].astype(F32)
    cc = c_ref[...].astype(F32)
    kk = k_ref[...].astype(F32)
    vv = v_ref[...].astype(F32)

    def columns(a, first, count):
        return jnp.concatenate(
            [a[:, (first + j) * 128:(first + j + 1) * 128] for j in range(count)], 0
        ).astype(BF16)

    dec_block = jnp.concatenate([dec, dec], 0).astype(BF16)
    for t in range(TP):
        at = slice(t * 128, (t + 1) * 128)
        bc_block = jnp.concatenate([bb[:, at], cc[:, at]], 0).astype(BF16)
        kv_send[t] = jnp.concatenate([kk[:, at], vv[:, at]], 0).astype(BF16)
        for l in range(LANES):
            d = l * TP + t
            a_send[d, 0:16, :] = columns(xx, t * 8 + l * 2, 2)
            a_send[d, 16:32, :] = bc_block
            a_send[d, 32:48, :] = dec_block
    a_recv[me] = a_send[me]
    kv_recv[tp] = kv_send[tp]
    for load in loads[8:10]:
        load.wait()
    qq = q_ref[...].astype(F32)
    for t in range(TP):
        q_send[t] = columns(qq, t * 4, 4)
    q_recv[me] = q_send[tp]
    tile_row = lax.broadcasted_iota(jnp.int32, (8, 128), 0)
    tile_lane = lax.broadcasted_iota(jnp.int32, (8, 128), 1)
    skips = jnp.zeros((8, 128), F32)
    for h in range(16):
        skips = jnp.where(tile_row * 2 + tile_lane // P_SIZE == h, skip_ref[h], skips)
    gain_ref[8:16, :] = skips
    g_recv[tp] = gain_ref[...]
    pl.semaphore_wait(barrier, PLANE - 1 + len(offsets))

    def copy(src, dst, send, recv, device):
        return pltpu.make_async_remote_copy(
            src_ref=src, dst_ref=dst, send_sem=send, recv_sem=recv,
            device_id=device, device_id_type=MESH,
        )

    def kv_copy(t, slot):
        return copy(kv_send.at[t], kv_recv.at[slot], kv_sem.at[0], kv_sem.at[1], (seq, t))

    def g_copy(t, slot):
        return copy(gain_ref, g_recv.at[slot], g_sem.at[0], g_sem.at[1], (seq, t))

    def a_copy(d, slot):
        return copy(a_send.at[d], a_recv.at[slot], a_sem.at[0], a_sem.at[1], place(d))

    def q_copy(d, slot):
        return copy(
            q_send.at[lax.rem(d, TP)], q_recv.at[slot], q_sem.at[0], q_sem.at[1], place(d)
        )

    def o_copy(d, slot):
        return copy(o_send.at[d], o_recv.at[slot], o_sem.at[0], o_sem.at[1], place(d))

    def y_copy(d, slot):
        return copy(y_send.at[d], y_recv.at[slot], y_sem.at[0], y_sem.at[1], place(d))

    def settle(buf, sem, count):
        part = buf.at[pl.ds(0, count)]
        pltpu.make_async_copy(part, part, sem).wait()

    def over_plane(act):
        def body(i, unused):
            act(lax.rem(me + i, PLANE))
            return unused

        lax.fori_loop(1, PLANE, body, 0)

    def over_tp(act):
        def body(i, unused):
            act(lax.rem(tp + i, TP))
            return unused

        lax.fori_loop(1, TP, body, 0)

    def hop(buf, ring, from_block, k, mark):
        block = lax.rem(z + Z + from_block, Z)
        return copy(
            buf.at[block], buf.at[block], z_ss.at[ring, mark], z_rs.at[ring, block], along(k)
        )

    def landed(buf, ring, k):
        hop(buf, ring, k, 1, 0).wait_recv()

    def wrapped(k):
        return lax.rem(z + Z + k, Z)

    def ups(r):
        return [(-2 * r, k, 2 * r + k - 1, (z >= 2 * r) & (z + k < Z)) for k in (2, 1)]

    def downs(r):
        block = wrapped(2 * r)
        return [
            (2 * r, -k, 7 + 2 * r + k, block <= (6 if k == 2 else 2 * r))
            for k in ((2, 1) if r < ROUNDS - 1 else (1,))
        ]

    hops = [one for r in range(ROUNDS) for one in ups(r) + downs(r)]

    def launch(buf, ring, which, causal):
        for from_block, k, mark, needed in which:
            if causal:
                pl.when(needed)(lambda f=from_block, k=k, m=mark: hop(buf, ring, f, k, m).start())
            else:
                hop(buf, ring, from_block, k, mark).start()

    def arrive(buf, ring, k, causal):
        if causal:
            block = wrapped(k)
            pl.when(block <= 6 if k in (2, 4, 6) else block < z)(lambda: landed(buf, ring, k))
        else:
            landed(buf, ring, k)

    def begin(buf, ring, causal):
        launch(buf, ring, ups(0) + downs(0), causal)

    def forward(buf, ring, r, causal):
        arrive(buf, ring, -2 * r, causal)
        launch(buf, ring, ups(r), causal)
        arrive(buf, ring, 2 * r, causal)
        launch(buf, ring, downs(r), causal)

    def sent(buf, ring, causal):
        for from_block, k, mark, needed in hops:
            if causal:
                pl.when(needed)(
                    lambda f=from_block, k=k, m=mark: hop(buf, ring, f, k, m).wait_send()
                )
            else:
                hop(buf, ring, from_block, k, mark).wait_send()

    others = (-1, 1, -3, 3, -5, 5, -7, 7, 8)

    over_tp(lambda t: kv_copy(t, tp).start())
    over_plane(lambda d: a_copy(d, me).start())
    begin(cache, 0, False)
    over_plane(lambda d: q_copy(d, me).start())
    over_tp(lambda t: g_copy(t, tp).start())

    forward(cache, 0, 1, False)

    settle(kv_recv, kv_sem.at[1], TP - 1)
    kv = kv_recv[...].astype(F32)
    fresh[z, 0:64, :] = kv[:, 0:8, :].reshape(64, DH).astype(BF16)
    fresh[z, 64:128, :] = kv[:, 8:16, :].reshape(64, DH).astype(BF16)
    begin(fresh, 1, True)
    forward(cache, 0, 2, False)
    settle(a_recv, a_sem.at[1], PLANE - 1)
    forward(fresh, 1, 1, True)

    def halves(first_row):
        part = a_recv[:, first_row:first_row + 16, :].astype(F32)
        return part[:, 0:8, :].reshape(SPAN, 128), part[:, 8:16, :].reshape(SPAN, 128)

    row = lax.broadcasted_iota(jnp.int32, (SPAN, SPAN), 0)
    col = lax.broadcasted_iota(jnp.int32, (SPAN, SPAN), 1)
    lower = row >= col
    ones = lower.astype(F32).astype(BF16)
    b_all, c_all = halves(16)
    b_all, c_all = b_all.astype(BF16), c_all.astype(BF16)
    mine = (
        lax.broadcasted_iota(jnp.int32, (128, SPAN), 0)
        == tp * 16 + lane * 4 + lax.broadcasted_iota(jnp.int32, (128, SPAN), 1) // P_SIZE
    )
    decay = dot(halves(32)[0].astype(BF16), mine.astype(F32).astype(BF16), 1, 0)
    decay = jnp.where(z * SPAN + row >= start_ref[0], decay, 0.0)
    d_all = decay.astype(BF16)
    x_all = jnp.concatenate(halves(0), 1) * in_weights(decay)
    cum = dot(ones, d_all, 1, 0)
    end = cum[SPAN - 1:SPAN, :]
    local = dot((x_all * jnp.exp(end - cum)).astype(BF16), b_all, 0, 0).astype(BF16)

    def log_rows(log):
        high = log.astype(BF16).astype(F32)
        return jnp.concatenate(
            [jnp.broadcast_to(high, (8, 128)), jnp.broadcast_to(log - high, (8, 128))], 0
        ).astype(BF16)

    for h in range(4):
        p1_send[h, 0:64, :] = local[h * P_SIZE:(h + 1) * P_SIZE, :]
        p1_send[h, 64:80, :] = log_rows(
            jnp.broadcast_to(end[:, h * P_SIZE:h * P_SIZE + 1], (1, 128))
        )
    p1_recv[member] = p1_send[member]

    def peer(k):
        return lax.rem(member + k, 4)

    def in_four(m):
        return ((four * 4 + m) * LANES + lane, tp)

    def p1_copy(m, slot):
        return copy(p1_send.at[m], p1_recv.at[slot], p1_sem.at[0], p1_sem.at[1], in_four(m))

    def p2_copy(f, slot):
        return copy(
            p2_send, p2_recv.at[slot], p2_ss.at[f], p2_rs.at[slot],
            ((f * 4 + member) * LANES + lane, tp),
        )

    def p3_copy(m, slot):
        return copy(p3_send.at[m], p3_recv.at[slot], p3_sem.at[0], p3_sem.at[1], in_four(m))

    for k in (1, 2, 3):
        p1_copy(peer(k), member).start()
    cum_ref[...] = cum
    forward(cache, 0, 3, False)

    x_all = x_all.astype(BF16)
    cum_t = dot(d_all, ones, 0, 1)
    pair = dot(c_all, b_all, 1, 1)
    first_half = lax.broadcasted_iota(jnp.int32, (SPAN, 128), 1) < P_SIZE
    for half in range(2):
        parts = []
        for j in (2 * half, 2 * half + 1):
            gap = cum[:, j * P_SIZE:j * P_SIZE + 1] - cum_t[j * P_SIZE:j * P_SIZE + 1, :]
            fade = jnp.where(lower, jnp.exp(jnp.where(lower, gap, 0.0)), 0.0)
            parts.append(
                dot((pair * fade).astype(BF16), x_all[:, half * 128:(half + 1) * 128], 1, 0)
            )
        y_ref[:, half * 128:(half + 1) * 128] = jnp.where(first_half, parts[0], parts[1])

    forward(fresh, 1, 2, True)

    settle(p1_recv, p1_sem.at[1], 3)

    def state_of(tile):
        tail = tile[64:80, :].astype(F32)
        return tile[0:64, :].astype(F32), tail[0:1, :] + tail[8:9, :]

    steps = [state_of(p1_recv[m]) for m in range(4)]
    total, total_log = steps[0]
    for add, log in steps[1:]:
        total, total_log = total * jnp.exp(log) + add, total_log + log
    p2_send[0:64, :] = total.astype(BF16)
    p2_send[64:80, :] = log_rows(total_log)
    for k in (1, 2, 3):
        pl.when(four + k < 4)(lambda k=k: p2_copy(four + k, four).start())

    def spread():
        for k in (1, 2, 3):
            pl.when(four - k >= 0)(lambda k=k: p2_copy(four, four - k).wait_recv())

        def lap(f, prior):
            add, log = state_of(p2_recv[f])
            return prior * jnp.exp(log) + add

        prior = lax.fori_loop(0, four, lap, init_ref[...])
        for m in range(4):
            p3_send[m] = prior.astype(BF16)
            if m < 3:
                add, log = state_of(p1_recv[m])
                prior = prior * jnp.exp(log) + add
        p3_recv[member] = p3_send[member]
        for k in (1, 2, 3):
            p3_copy(peer(k), member).start()

    loads[10].wait()
    pl.when(four == 0)(spread)
    forward(fresh, 1, 3, True)

    key_at = lax.broadcasted_iota(jnp.int32, (1, KEYS), 1)
    key_place = (key_at // 64) * SPAN + lane * 64 + lax.rem(key_at, 64)
    row_at = lax.broadcasted_iota(jnp.int32, (UNIT, 1), 0)

    def part(u, buf, usable):
        queries = q_recv[pl.ds(u * 8, 8)].reshape(UNIT, DH)
        keys = buf[:, 0:64, :].reshape(KEYS, DH)
        values = buf[:, 64:128, :].reshape(KEYS, DH)
        scores = jnp.where(usable, dot(queries, keys, 1, 1) * SCALE, LOW)
        top = jnp.max(scores, axis=1, keepdims=True)
        weights = jnp.exp(scores - top)
        total = jnp.sum(weights, axis=1, keepdims=True)
        return top, total, dot(weights.astype(BF16), values, 1, 0)

    settle(q_recv, q_sem.at[1], PLANE - 1)
    for k in others:
        arrive(cache, 0, k, False)
    cached = key_place < length_ref[0]
    for u in range(ROWS // UNIT):
        top, weight, mixed = part(u, cache, cached)
        m1[u * UNIT:(u + 1) * UNIT, :] = top
        l1[u * UNIT:(u + 1) * UNIT, :] = weight
        o1[u * UNIT:(u + 1) * UNIT, :] = mixed

    pl.when(four > 0)(spread)

    for k in others:
        arrive(fresh, 1, k, True)
    spot = (
        lax.broadcasted_iota(jnp.int32, (1, 32, 128), 1)
        == lax.broadcasted_iota(jnp.int32, (1, 32, 128), 2)
    ).astype(F32)
    spot_row = lax.broadcasted_iota(jnp.int32, (8, 16, 128), 1)

    def unit(i, unused):
        u = lax.rem(lane + 1 + i, LANES)
        query_place = z * SPAN + u * 64 + (row_at // 32) * 8 + lax.rem(row_at, 8)
        usable = (key_place >= start_ref[0]) & (key_place <= query_place)
        top, weight, mixed = part(u, fresh, usable)
        rows = pl.ds(pl.multiple_of(u * UNIT, UNIT), UNIT)
        top1, weight1 = m1[rows, :], l1[rows, :]
        both = jnp.maximum(top, top1)
        by, by1 = jnp.exp(top - both), jnp.exp(top1 - both)
        weight = weight * by + weight1 * by1
        mixed = (mixed * by + o1[rows, :] * by1) / weight
        o_send[pl.ds(u * 8, 8), 0:32, :] = mixed.astype(BF16).reshape(8, 32, DH)
        size = jnp.broadcast_to(both + jnp.log(weight), (UNIT, 128)).reshape(8, 32, 128)
        size = jnp.sum(size * spot, axis=1, keepdims=True)
        high = size.astype(BF16).astype(F32)
        middle = (size - high).astype(BF16).astype(F32)
        o_send[pl.ds(u * 8, 8), 32:48, :] = jnp.where(
            spot_row < 8, high, jnp.where(spot_row < 15, middle, size - high - middle)
        ).astype(BF16)
        for n in range(1, TP):
            o_copy(u * TP + lax.rem(tp + n, TP), me).start()
        pl.when(u != lane)(lambda: o_copy(u * TP + tp, me).start())
        return unused

    for i in range(LANES):
        unit(i, 0)
    o_recv[me] = o_send[me]

    settle(p3_recv, p3_sem.at[1], 3)
    incoming = p3_recv[...].reshape(SPAN, 128)
    y = y_ref[...] + jnp.exp(cum_ref[...]) * dot(c_all, incoming, 1, 1)
    y_send[...] = jnp.concatenate(
        [y[:, 0:128].reshape(PLANE, 8, 128), y[:, 128:256].reshape(PLANE, 8, 128)], 1
    ).astype(BF16)
    y_recv[me] = y_send[me]
    over_plane(lambda d: y_copy(d, me).start())

    settle(o_recv, o_sem.at[1], PLANE - 1)
    for t in range(TP):
        sizes = []
        for l in range(LANES):
            tile = o_recv[l * TP + t, 32:48, :].astype(F32)
            line = tile[0:1, :] + tile[8:9, :] + tile[15:16, :]
            sizes.append(jnp.sum(line * spot[0], axis=1, keepdims=True))
        most = jnp.maximum(jnp.maximum(sizes[0], sizes[1]), jnp.maximum(sizes[2], sizes[3]))
        shares = [jnp.exp(size - most) for size in sizes]
        whole = shares[0] + shares[1] + shares[2] + shares[3]
        out = sum(
            share * o_recv[l * TP + t, 0:32, :].astype(F32) for l, share in enumerate(shares)
        ) / whole
        for h in range(4):
            at = (t * 4 + h) * 128
            attn_ref[:, at:at + 128] = out[h * 8:(h + 1) * 8, :].astype(BF16)

    settle(g_recv, g_sem.at[1], TP - 1)
    loads[11].wait()
    settle(y_recv, y_sem.at[1], PLANE - 1)
    for t in range(TP):
        gated, squares = [], 0.0
        for l in range(LANES):
            y_part = y_recv[l * TP + t].astype(F32)
            for half in range(2):
                r = l * 2 + half
                at = t * 1024 + r * 128
                gate = gate_ref[:, at:at + 128].astype(F32)
                value = y_part[half * 8:(half + 1) * 8, :] + g_recv[
                    t, 8 + r:9 + r, :
                ] * x_ref[:, at:at + 128].astype(F32)
                value = value * (gate / (1.0 + jnp.exp(-gate)))
                squares = squares + value * value
                gated.append(value)
        scale = lax.rsqrt(jnp.sum(squares, axis=1, keepdims=True) * (1.0 / 1024) + 1e-5)
        for r in range(8):
            at = t * 1024 + r * 128
            ssm_ref[:, at:at + 128] = (gated[r] * scale * g_recv[t, r:r + 1, :]).astype(BF16)

    settle(kv_recv, kv_sem.at[0], TP - 1)
    settle(g_recv, g_sem.at[0], TP - 1)
    settle(a_recv, a_sem.at[0], PLANE - 1)
    settle(q_recv, q_sem.at[0], PLANE - 1)
    settle(o_recv, o_sem.at[0], PLANE - 1)
    settle(y_recv, y_sem.at[0], PLANE - 1)
    settle(p1_recv, p1_sem.at[0], 3)
    settle(p3_recv, p3_sem.at[0], 3)
    sent(cache, 0, False)
    sent(fresh, 1, True)
    for k in (1, 2, 3):
        pl.when(four + k < 4)(lambda k=k: p2_copy(four + k, four).wait_send())


def local(
    query, key_new, value_new, ssm_input, ssm_gate, ssm_b, ssm_c, log_decay,
    key_cache, value_cache, init_state, skip_gain, norm_gain, cache_length, span_start,
):
    vmem = pl.BlockSpec(memory_space=pltpu.VMEM)
    smem = pl.BlockSpec(memory_space=pltpu.SMEM)
    hbm = pl.BlockSpec(memory_space=pltpu.HBM)
    dma = pltpu.SemaphoreType.DMA
    return pl.pallas_call(
        kernel,
        out_shape=(
            jax.ShapeDtypeStruct((8, 4096), BF16),
            jax.ShapeDtypeStruct((8, 8192), BF16),
        ),
        in_specs=[smem] * 3 + [hbm] * 12,
        out_specs=(vmem, vmem),
        scratch_shapes=[
            pltpu.VMEM((8, 4096), BF16),
            pltpu.VMEM((8, 1024), BF16),
            pltpu.VMEM((8, 1024), BF16),
            pltpu.VMEM((8, 8192), BF16),
            pltpu.VMEM((8, 128), BF16),
            pltpu.VMEM((8, 1024), BF16),
            pltpu.VMEM((8, 1024), BF16),
            pltpu.VMEM((64, 128), BF16),
            pltpu.VMEM((64, 128), BF16),
            pltpu.VMEM((64, 128), F32),
            pltpu.VMEM((16, 128), F32),
            pltpu.VMEM((8, 8192), BF16),
            pltpu.VMEM((PLANE, 48, 128), BF16),
            pltpu.VMEM((PLANE, 48, 128), BF16),
            pltpu.VMEM((TP, 32, 128), BF16),
            pltpu.VMEM((PLANE, 32, 128), BF16),
            pltpu.VMEM((TP, 16, 128), BF16),
            pltpu.VMEM((TP, 16, 128), BF16),
            pltpu.VMEM((TP, 16, 128), F32),
            pltpu.VMEM((Z, 128, DH), BF16),
            pltpu.VMEM((Z, 128, DH), BF16),
            pltpu.VMEM((4, 80, 128), BF16),
            pltpu.VMEM((4, 80, 128), BF16),
            pltpu.VMEM((80, 128), BF16),
            pltpu.VMEM((4, 80, 128), BF16),
            pltpu.VMEM((4, 64, 128), BF16),
            pltpu.VMEM((4, 64, 128), BF16),
            pltpu.VMEM((SPAN, SPAN), F32),
            pltpu.VMEM((SPAN, SPAN), F32),
            pltpu.VMEM((ROWS, DH), F32),
            pltpu.VMEM((ROWS, 1), F32),
            pltpu.VMEM((ROWS, 1), F32),
            pltpu.VMEM((PLANE, 48, 128), BF16),
            pltpu.VMEM((PLANE, 48, 128), BF16),
            pltpu.VMEM((PLANE, 16, 128), BF16),
            pltpu.VMEM((PLANE, 16, 128), BF16),
            dma((12,)), dma((2,)), dma((2,)), dma((2,)), dma((2,)),
            dma((2, 16)), dma((2, Z)),
            dma((2,)), dma((4,)), dma((4,)), dma((2,)), dma((2,)), dma((2,)),
        ],
        compiler_params=pltpu.CompilerParams(
            collective_id=0, has_side_effects=True, vmem_limit_bytes=56 * 1024 * 1024
        ),
        name="mixers",
    )(
        cache_length, span_start, skip_gain,
        query, key_new, value_new, ssm_input, log_decay, ssm_b, ssm_c,
        key_cache, value_cache, init_state, norm_gain.reshape(8, 128), ssm_gate,
    )


def solution(mesh):
    rows = P(("seq", "tp"), None)
    placed = (rows,) * 8 + (
        P("seq", "tp"),
        P("seq", "tp"),
        P("tp", None, None),
        P("tp"),
        P("tp"),
        P(),
        P(),
    )
    return jax.shard_map(
        local, mesh=mesh, in_specs=placed, out_specs=(rows, rows), check_vma=False
    )
```

```python
import jax
import jax.numpy as jnp
from jax import lax
from jax.experimental import pallas as pl
from jax.experimental.pallas import tpu as pltpu
from jax.sharding import PartitionSpec as P

Z = 16
LANES = 4
TP = 8
PLANE = LANES * TP
DH = 128
P_SIZE = 64
SPAN = 256
KEYS = 1024
ROWS = 1024
UNIT = 256
REACH = 4
ROUNDS = 4
SCALE = 128.0 ** -0.5
LOW = -1e30
MESH = pl.DeviceIdType.MESH
F32 = jnp.float32
BF16 = jnp.bfloat16


def dot(a, b, ca, cb):
    return lax.dot_general(a, b, (((ca,), (cb,)), ((), ())), preferred_element_type=F32)


def in_weights(decay):
    u = 2.0 * decay
    series = 1.0 + u * (1.0 / 12)
    for k in range(11, 1, -1):
        series = 1.0 + u * (1.0 / k) * series
    return jnp.sqrt(jnp.where(u < -1.0, 1.0 - jnp.exp(u), -u * series))


def kernel(
    length_ref, start_ref, skip_ref,
    q_hbm, k_hbm, v_hbm, x_hbm, dec_hbm, b_hbm, c_hbm, kc_hbm, vc_hbm, init_hbm, norm_hbm, gate_hbm,
    attn_ref, ssm_ref,
    q_ref, k_ref, v_ref, x_ref, dec_ref, b_ref, c_ref, kc_ref, vc_ref, init_ref, gain_ref, gate_ref,
    a_send, a_recv, q_send, q_recv, kv_send, kv_recv, g_recv, cache, fresh,
    p1_send, p1_recv, p2_send, p2_recv, p3_send, p3_recv,
    cum_ref, y_ref, gates, direct, o1, m1, l1, o_send, o_recv, y_send, y_recv,
    in_sem, a_sem, q_sem, kv_sem, g_sem, z_ss, z_rs, p1_sem, p2_ss, p2_rs, p3_sem, o_sem, y_sem,
):
    seq, tp = lax.axis_index("seq"), lax.axis_index("tp")
    z, lane = seq // LANES, lax.rem(seq, LANES)
    me = lane * TP + tp
    four, member = z // 4, lax.rem(z, 4)

    loads = [
        pltpu.make_async_copy(src, dst, in_sem.at[n])
        for n, (src, dst) in enumerate(
            (
                (x_hbm, x_ref), (b_hbm, b_ref), (c_hbm, c_ref), (dec_hbm, dec_ref),
                (k_hbm, k_ref), (v_hbm, v_ref), (kc_hbm, kc_ref), (vc_hbm, vc_ref),
                (q_hbm, q_ref), (norm_hbm, gain_ref.at[pl.ds(0, 8)]),
                (init_hbm.at[lane * 4 + member], init_ref), (gate_hbm, gate_ref),
            )
        )
    ]
    for load in loads:
        load.start()
    fresh[...] = jnp.zeros_like(fresh)

    def place(d):
        return (z * LANES + d // TP, lax.rem(d, TP))

    def along(k):
        return (lax.rem(z + Z + k, Z) * LANES + lane, tp)

    barrier = pltpu.get_barrier_semaphore()

    def greet(i, unused):
        pl.semaphore_signal(
            barrier, inc=1, device_id=place(lax.rem(me + i, PLANE)), device_id_type=MESH
        )
        return unused

    offsets = [k for k in range(-REACH, REACH + 1) if k] + [8]
    for k in offsets:
        pl.semaphore_signal(barrier, inc=1, device_id=along(k), device_id_type=MESH)
    lax.fori_loop(1, PLANE, greet, 0)

    for load in loads[:8]:
        load.wait()
    cache[z, 0:64, :] = kc_ref[...]
    cache[z, 64:128, :] = vc_ref[...]
    xx = x_ref[...].astype(F32)
    dec = dec_ref[...].astype(F32)
    bb = b_ref[...].astype(F32)
    cc = c_ref[...].astype(F32)
    kk = k_ref[...].astype(F32)
    vv = v_ref[...].astype(F32)

    def columns(a, first, count):
        return jnp.concatenate(
            [a[:, (first + j) * 128:(first + j + 1) * 128] for j in range(count)], 0
        ).astype(BF16)

    place_at = (seq * TP + tp) * 8 + lax.broadcasted_iota(jnp.int32, (8, 128), 0)
    dec = jnp.where(place_at >= start_ref[0], dec, 0.0)
    dec_block = jnp.concatenate([dec, in_weights(dec)], 0).astype(BF16)
    for t in range(TP):
        at = slice(t * 128, (t + 1) * 128)
        bc_block = jnp.concatenate([bb[:, at], cc[:, at]], 0).astype(BF16)
        kv_send[t] = jnp.concatenate([kk[:, at], vv[:, at]], 0).astype(BF16)
        for l in range(LANES):
            d = l * TP + t
            a_send[d, 0:16, :] = columns(xx, t * 8 + l * 2, 2)
            a_send[d, 16:32, :] = bc_block
            a_send[d, 32:48, :] = dec_block
    a_recv[me] = a_send[me]
    kv_recv[tp] = kv_send[tp]
    for load in loads[8:10]:
        load.wait()
    qq = q_ref[...].astype(F32)
    for t in range(TP):
        q_send[t] = columns(qq, t * 4, 4)
    q_recv[me] = q_send[tp]
    tile_row = lax.broadcasted_iota(jnp.int32, (8, 128), 0)
    tile_lane = lax.broadcasted_iota(jnp.int32, (8, 128), 1)
    skips = jnp.zeros((8, 128), F32)
    for h in range(16):
        skips = jnp.where(tile_row * 2 + tile_lane // P_SIZE == h, skip_ref[h], skips)
    gain_ref[8:16, :] = skips
    g_recv[tp] = gain_ref[...]
    pl.semaphore_wait(barrier, PLANE - 1 + len(offsets))

    def copy(src, dst, send, recv, device):
        return pltpu.make_async_remote_copy(
            src_ref=src, dst_ref=dst, send_sem=send, recv_sem=recv,
            device_id=device, device_id_type=MESH,
        )

    def kv_copy(t, slot):
        return copy(kv_send.at[t], kv_recv.at[slot], kv_sem.at[0], kv_sem.at[1], (seq, t))

    def g_copy(t, slot):
        return copy(gain_ref, g_recv.at[slot], g_sem.at[0], g_sem.at[1], (seq, t))

    def a_copy(d, slot):
        return copy(a_send.at[d], a_recv.at[slot], a_sem.at[0], a_sem.at[1], place(d))

    def q_copy(d, slot):
        return copy(
            q_send.at[lax.rem(d, TP)], q_recv.at[slot], q_sem.at[0], q_sem.at[1], place(d)
        )

    def o_copy(d, slot):
        return copy(o_send.at[d], o_recv.at[slot], o_sem.at[0], o_sem.at[1], place(d))

    def y_copy(d, slot):
        return copy(y_send.at[d], y_recv.at[slot], y_sem.at[0], y_sem.at[1], place(d))

    def settle(buf, sem, count):
        part = buf.at[pl.ds(0, count)]
        pltpu.make_async_copy(part, part, sem).wait()

    def over_plane(act):
        def body(i, unused):
            act(lax.rem(me + i, PLANE))
            return unused

        lax.fori_loop(1, PLANE, body, 0)

    def over_tp(act):
        def body(i, unused):
            act(lax.rem(tp + i, TP))
            return unused

        lax.fori_loop(1, TP, body, 0)

    def hop(buf, ring, from_block, k, mark):
        block = lax.rem(z + Z + from_block, Z)
        return copy(
            buf.at[block], buf.at[block], z_ss.at[ring, mark], z_rs.at[ring, block], along(k)
        )

    def landed(buf, ring, k):
        hop(buf, ring, k, 1, 0).wait_recv()

    def wrapped(k):
        return lax.rem(z + Z + k, Z)

    def ups(r):
        return [(-2 * r, k, 2 * r + k - 1, (z >= 2 * r) & (z + k < Z)) for k in (2, 1)]

    def downs(r):
        block = wrapped(2 * r)
        return [
            (2 * r, -k, 7 + 2 * r + k, block <= (6 if k == 2 else 2 * r))
            for k in ((2, 1) if r < ROUNDS - 1 else (1,))
        ]

    hops = [one for r in range(ROUNDS) for one in ups(r) + downs(r)]

    def launch(buf, ring, which, causal):
        for from_block, k, mark, needed in which:
            if causal:
                pl.when(needed)(lambda f=from_block, k=k, m=mark: hop(buf, ring, f, k, m).start())
            else:
                hop(buf, ring, from_block, k, mark).start()

    def arrive(buf, ring, k, causal):
        if causal:
            block = wrapped(k)
            pl.when(block <= 6 if k in (2, 4, 6) else block < z)(lambda: landed(buf, ring, k))
        else:
            landed(buf, ring, k)

    def begin(buf, ring, causal):
        launch(buf, ring, ups(0) + downs(0), causal)

    def forward(buf, ring, r, causal):
        arrive(buf, ring, -2 * r, causal)
        launch(buf, ring, ups(r), causal)
        arrive(buf, ring, 2 * r, causal)
        launch(buf, ring, downs(r), causal)

    def sent(buf, ring, causal):
        for from_block, k, mark, needed in hops:
            if causal:
                pl.when(needed)(
                    lambda f=from_block, k=k, m=mark: hop(buf, ring, f, k, m).wait_send()
                )
            else:
                hop(buf, ring, from_block, k, mark).wait_send()

    others = (-1, 1, -3, 3, -5, 5, -7, 7, 8)

    over_tp(lambda t: kv_copy(t, tp).start())
    begin(cache, 0, False)
    over_plane(lambda d: a_copy(d, me).start())
    over_plane(lambda d: q_copy(d, me).start())
    over_tp(lambda t: g_copy(t, tp).start())

    forward(cache, 0, 1, False)

    settle(kv_recv, kv_sem.at[1], TP - 1)
    kv = kv_recv[...].astype(F32)
    fresh[z, 0:64, :] = kv[:, 0:8, :].reshape(64, DH).astype(BF16)
    fresh[z, 64:128, :] = kv[:, 8:16, :].reshape(64, DH).astype(BF16)
    begin(fresh, 1, True)
    forward(cache, 0, 2, False)
    row = lax.broadcasted_iota(jnp.int32, (SPAN, SPAN), 0)
    col = lax.broadcasted_iota(jnp.int32, (SPAN, SPAN), 1)
    lower = row >= col
    ones = lower.astype(F32).astype(BF16)
    mine = (
        lax.broadcasted_iota(jnp.int32, (128, SPAN), 0)
        == tp * 16 + lane * 4 + lax.broadcasted_iota(jnp.int32, (128, SPAN), 1) // P_SIZE
    )
    mine = mine.astype(F32).astype(BF16)
    forward(fresh, 1, 1, True)
    settle(a_recv, a_sem.at[1], PLANE - 1)

    def halves(first_row):
        part = a_recv[:, first_row:first_row + 16, :].astype(F32)
        return part[:, 0:8, :].reshape(SPAN, 128), part[:, 8:16, :].reshape(SPAN, 128)

    b_all, c_all = halves(16)
    b_all, c_all = b_all.astype(BF16), c_all.astype(BF16)
    decays, weights = halves(32)
    d_all = dot(decays.astype(BF16), mine, 1, 0).astype(BF16)
    x_all = jnp.concatenate(halves(0), 1) * dot(weights.astype(BF16), mine, 1, 0)
    cum = dot(ones, d_all, 1, 0)
    end = cum[SPAN - 1:SPAN, :]
    local = dot((x_all * jnp.exp(end - cum)).astype(BF16), b_all, 0, 0).astype(BF16)

    def log_rows(log):
        high = log.astype(BF16).astype(F32)
        return jnp.concatenate(
            [jnp.broadcast_to(high, (8, 128)), jnp.broadcast_to(log - high, (8, 128))], 0
        ).astype(BF16)

    for h in range(4):
        p1_send[h, 0:64, :] = local[h * P_SIZE:(h + 1) * P_SIZE, :]
        p1_send[h, 64:80, :] = log_rows(
            jnp.broadcast_to(end[:, h * P_SIZE:h * P_SIZE + 1], (1, 128))
        )
    p1_recv[member] = p1_send[member]

    def peer(k):
        return lax.rem(member + k, 4)

    def in_four(m):
        return ((four * 4 + m) * LANES + lane, tp)

    def p1_copy(m, slot):
        return copy(p1_send.at[m], p1_recv.at[slot], p1_sem.at[0], p1_sem.at[1], in_four(m))

    def p2_copy(f, slot):
        return copy(
            p2_send, p2_recv.at[slot], p2_ss.at[f], p2_rs.at[slot],
            ((f * 4 + member) * LANES + lane, tp),
        )

    def p3_copy(m, slot):
        return copy(p3_send.at[m], p3_recv.at[slot], p3_sem.at[0], p3_sem.at[1], in_four(m))

    for k in (1, 2, 3):
        p1_copy(peer(k), member).start()
    cum_ref[...] = cum
    forward(cache, 0, 3, False)

    x_all = x_all.astype(BF16)
    cum_t = dot(d_all, ones, 0, 1)
    pair = dot(c_all, b_all, 1, 1)
    first_half = lax.broadcasted_iota(jnp.int32, (SPAN, 128), 1) < P_SIZE
    for half in range(2):
        parts = []
        for j in (2 * half, 2 * half + 1):
            gap = cum[:, j * P_SIZE:j * P_SIZE + 1] - cum_t[j * P_SIZE:j * P_SIZE + 1, :]
            fade = jnp.where(lower, jnp.exp(jnp.where(lower, gap, 0.0)), 0.0)
            parts.append(
                dot((pair * fade).astype(BF16), x_all[:, half * 128:(half + 1) * 128], 1, 0)
            )
        y_ref[:, half * 128:(half + 1) * 128] = jnp.where(first_half, parts[0], parts[1])

    forward(fresh, 1, 2, True)

    settle(p1_recv, p1_sem.at[1], 3)

    def state_of(tile):
        tail = tile[64:80, :].astype(F32)
        return tile[0:64, :].astype(F32), tail[0:1, :] + tail[8:9, :]

    steps = [state_of(p1_recv[m]) for m in range(4)]
    total, total_log = steps[0]
    for add, log in steps[1:]:
        total, total_log = total * jnp.exp(log) + add, total_log + log
    p2_send[0:64, :] = total.astype(BF16)
    p2_send[64:80, :] = log_rows(total_log)
    for k in (1, 2, 3):
        pl.when(four + k < 4)(lambda k=k: p2_copy(four + k, four).start())

    def spread():
        for k in (1, 2, 3):
            pl.when(four - k >= 0)(lambda k=k: p2_copy(four, four - k).wait_recv())

        def lap(f, prior):
            add, log = state_of(p2_recv[f])
            return prior * jnp.exp(log) + add

        prior = lax.fori_loop(0, four, lap, init_ref[...])
        for m in range(4):
            p3_send[m] = prior.astype(BF16)
            if m < 3:
                add, log = state_of(p1_recv[m])
                prior = prior * jnp.exp(log) + add
        p3_recv[member] = p3_send[member]
        for k in (1, 2, 3):
            p3_copy(peer(k), member).start()

    loads[10].wait()
    pl.when(four == 0)(spread)

    key_at = lax.broadcasted_iota(jnp.int32, (1, KEYS), 1)
    key_place = (key_at // 64) * SPAN + lane * 64 + lax.rem(key_at, 64)
    row_at = lax.broadcasted_iota(jnp.int32, (UNIT, 1), 0)

    def part(u, buf, usable, blocks=Z):
        queries = q_recv[pl.ds(u * 8, 8)].reshape(UNIT, DH)
        keys = buf[0:blocks, 0:64, :].reshape(blocks * 64, DH)
        values = buf[0:blocks, 64:128, :].reshape(blocks * 64, DH)
        scores = jnp.where(usable, dot(queries, keys, 1, 1) * SCALE, LOW)
        top = jnp.max(scores, axis=1, keepdims=True)
        weights = jnp.exp(scores - top)
        total = jnp.sum(weights, axis=1, keepdims=True)
        return top, total, dot(weights.astype(BF16), values, 1, 0)

    settle(q_recv, q_sem.at[1], PLANE - 1)
    for k in others:
        arrive(cache, 0, k, False)
    cached = key_place < length_ref[0]
    for u in range(ROWS // UNIT):
        top, weight, mixed = part(u, cache, cached)
        m1[u * UNIT:(u + 1) * UNIT, :] = top
        l1[u * UNIT:(u + 1) * UNIT, :] = weight
        o1[u * UNIT:(u + 1) * UNIT, :] = mixed
        if u == 1:
            forward(fresh, 1, 3, True)

    pl.when(four > 0)(spread)

    for k in others:
        arrive(fresh, 1, k, True)
    spot = (
        lax.broadcasted_iota(jnp.int32, (1, 32, 128), 1)
        == lax.broadcasted_iota(jnp.int32, (1, 32, 128), 2)
    ).astype(F32)
    spot_row = lax.broadcasted_iota(jnp.int32, (8, 16, 128), 1)

    def unit(i, blocks):
        u = lax.rem(lane + 1 + i, LANES)
        query_place = z * SPAN + u * 64 + (row_at // 32) * 8 + lax.rem(row_at, 8)
        places = key_place[:, 0:blocks * 64]
        usable = (places >= start_ref[0]) & (places <= query_place)
        top, weight, mixed = part(u, fresh, usable, blocks)
        rows = pl.ds(pl.multiple_of(u * UNIT, UNIT), UNIT)
        top1, weight1 = m1[rows, :], l1[rows, :]
        both = jnp.maximum(top, top1)
        by, by1 = jnp.exp(top - both), jnp.exp(top1 - both)
        weight = weight * by + weight1 * by1
        mixed = (mixed * by + o1[rows, :] * by1) / weight
        o_send[pl.ds(u * 8, 8), 0:32, :] = mixed.astype(BF16).reshape(8, 32, DH)
        size = jnp.broadcast_to(both + jnp.log(weight), (UNIT, 128)).reshape(8, 32, 128)
        size = jnp.sum(size * spot, axis=1, keepdims=True)
        high = size.astype(BF16).astype(F32)
        middle = (size - high).astype(BF16).astype(F32)
        o_send[pl.ds(u * 8, 8), 32:48, :] = jnp.where(
            spot_row < 8, high, jnp.where(spot_row < 15, middle, size - high - middle)
        ).astype(BF16)
        for n in range(1, TP):
            o_copy(u * TP + lax.rem(tp + n, TP), me).start()
        pl.when(u != lane)(lambda: o_copy(u * TP + tp, me).start())

    def units(blocks):
        for i in range(LANES):
            unit(i, blocks)

    pl.when(z < Z // 2)(lambda: units(Z // 2))
    pl.when(z >= Z // 2)(lambda: units(Z))
    o_recv[me] = o_send[me]

    settle(p3_recv, p3_sem.at[1], 3)
    incoming = p3_recv[...].reshape(SPAN, 128)
    y = y_ref[...] + jnp.exp(cum_ref[...]) * dot(c_all, incoming, 1, 1)
    y_send[...] = jnp.concatenate(
        [y[:, 0:128].reshape(PLANE, 8, 128), y[:, 128:256].reshape(PLANE, 8, 128)], 1
    ).astype(BF16)
    y_recv[me] = y_send[me]
    over_plane(lambda d: y_copy(d, me).start())

    settle(g_recv, g_sem.at[1], TP - 1)
    loads[11].wait()
    for t in range(TP):
        for r in range(8):
            at = slice(t * 1024 + r * 128, t * 1024 + (r + 1) * 128)
            gate = gate_ref[:, at].astype(F32)
            gates[:, at] = gate / (1.0 + jnp.exp(-gate))
            direct[:, at] = g_recv[t, 8 + r:9 + r, :] * x_ref[:, at].astype(F32)
    settle(o_recv, o_sem.at[1], PLANE - 1)
    for t in range(TP):
        sizes = []
        for l in range(LANES):
            tile = o_recv[l * TP + t, 32:48, :].astype(F32)
            line = tile[0:1, :] + tile[8:9, :] + tile[15:16, :]
            sizes.append(jnp.sum(line * spot[0], axis=1, keepdims=True))
        most = jnp.maximum(jnp.maximum(sizes[0], sizes[1]), jnp.maximum(sizes[2], sizes[3]))
        shares = [jnp.exp(size - most) for size in sizes]
        whole = shares[0] + shares[1] + shares[2] + shares[3]
        out = sum(
            share * o_recv[l * TP + t, 0:32, :].astype(F32) for l, share in enumerate(shares)
        ) / whole
        for h in range(4):
            at = (t * 4 + h) * 128
            attn_ref[:, at:at + 128] = out[h * 8:(h + 1) * 8, :].astype(BF16)

    settle(y_recv, y_sem.at[1], PLANE - 1)
    for t in range(TP):
        gated, squares = [], 0.0
        for l in range(LANES):
            y_part = y_recv[l * TP + t].astype(F32)
            for half in range(2):
                r = l * 2 + half
                at = t * 1024 + r * 128
                value = y_part[half * 8:(half + 1) * 8, :] + direct[:, at:at + 128]
                value = value * gates[:, at:at + 128]
                squares = squares + value * value
                gated.append(value)
        scale = lax.rsqrt(jnp.sum(squares, axis=1, keepdims=True) * (1.0 / 1024) + 1e-5)
        for r in range(8):
            at = t * 1024 + r * 128
            ssm_ref[:, at:at + 128] = (gated[r] * scale * g_recv[t, r:r + 1, :]).astype(BF16)

    settle(kv_recv, kv_sem.at[0], TP - 1)
    settle(g_recv, g_sem.at[0], TP - 1)
    settle(a_recv, a_sem.at[0], PLANE - 1)
    settle(q_recv, q_sem.at[0], PLANE - 1)
    settle(o_recv, o_sem.at[0], PLANE - 1)
    settle(y_recv, y_sem.at[0], PLANE - 1)
    settle(p1_recv, p1_sem.at[0], 3)
    settle(p3_recv, p3_sem.at[0], 3)
    sent(cache, 0, False)
    sent(fresh, 1, True)
    for k in (1, 2, 3):
        pl.when(four + k < 4)(lambda k=k: p2_copy(four + k, four).wait_send())


def local(
    query, key_new, value_new, ssm_input, ssm_gate, ssm_b, ssm_c, log_decay,
    key_cache, value_cache, init_state, skip_gain, norm_gain, cache_length, span_start,
):
    vmem = pl.BlockSpec(memory_space=pltpu.VMEM)
    smem = pl.BlockSpec(memory_space=pltpu.SMEM)
    hbm = pl.BlockSpec(memory_space=pltpu.HBM)
    dma = pltpu.SemaphoreType.DMA
    return pl.pallas_call(
        kernel,
        out_shape=(
            pltpu.VMEM((8, 4096), BF16),
            pltpu.VMEM((8, 8192), BF16),
        ),
        in_specs=[smem] * 3 + [hbm] * 12,
        out_specs=(vmem, vmem),
        scratch_shapes=[
            pltpu.VMEM((8, 4096), BF16),
            pltpu.VMEM((8, 1024), BF16),
            pltpu.VMEM((8, 1024), BF16),
            pltpu.VMEM((8, 8192), BF16),
            pltpu.VMEM((8, 128), BF16),
            pltpu.VMEM((8, 1024), BF16),
            pltpu.VMEM((8, 1024), BF16),
            pltpu.VMEM((64, 128), BF16),
            pltpu.VMEM((64, 128), BF16),
            pltpu.VMEM((64, 128), F32),
            pltpu.VMEM((16, 128), F32),
            pltpu.VMEM((8, 8192), BF16),
            pltpu.VMEM((PLANE, 48, 128), BF16),
            pltpu.VMEM((PLANE, 48, 128), BF16),
            pltpu.VMEM((TP, 32, 128), BF16),
            pltpu.VMEM((PLANE, 32, 128), BF16),
            pltpu.VMEM((TP, 16, 128), BF16),
            pltpu.VMEM((TP, 16, 128), BF16),
            pltpu.VMEM((TP, 16, 128), F32),
            pltpu.VMEM((Z, 128, DH), BF16),
            pltpu.VMEM((Z, 128, DH), BF16),
            pltpu.VMEM((4, 80, 128), BF16),
            pltpu.VMEM((4, 80, 128), BF16),
            pltpu.VMEM((80, 128), BF16),
            pltpu.VMEM((4, 80, 128), BF16),
            pltpu.VMEM((4, 64, 128), BF16),
            pltpu.VMEM((4, 64, 128), BF16),
            pltpu.VMEM((SPAN, SPAN), F32),
            pltpu.VMEM((SPAN, SPAN), F32),
            pltpu.VMEM((8, 8192), F32),
            pltpu.VMEM((8, 8192), F32),
            pltpu.VMEM((ROWS, DH), F32),
            pltpu.VMEM((ROWS, 1), F32),
            pltpu.VMEM((ROWS, 1), F32),
            pltpu.VMEM((PLANE, 48, 128), BF16),
            pltpu.VMEM((PLANE, 48, 128), BF16),
            pltpu.VMEM((PLANE, 16, 128), BF16),
            pltpu.VMEM((PLANE, 16, 128), BF16),
            dma((12,)), dma((2,)), dma((2,)), dma((2,)), dma((2,)),
            dma((2, 16)), dma((2, Z)),
            dma((2,)), dma((4,)), dma((4,)), dma((2,)), dma((2,)), dma((2,)),
        ],
        compiler_params=pltpu.CompilerParams(
            collective_id=0, has_side_effects=True, vmem_limit_bytes=56 * 1024 * 1024
        ),
        name="mixers",
    )(
        cache_length, span_start, skip_gain,
        query, key_new, value_new, ssm_input, log_decay, ssm_b, ssm_c,
        key_cache, value_cache, init_state, norm_gain.reshape(8, 128), ssm_gate,
    )


def solution(mesh):
    rows = P(("seq", "tp"), None)
    placed = (rows,) * 8 + (
        P("seq", "tp"),
        P("seq", "tp"),
        P("tp", None, None),
        P("tp"),
        P("tp"),
        P(),
        P(),
    )
    return jax.shard_map(
        local, mesh=mesh, in_specs=placed, out_specs=(rows, rows), check_vma=False
    )
```

```python
import jax
import jax.numpy as jnp
from jax import lax
from jax.experimental import pallas as pl
from jax.experimental.pallas import tpu as pltpu
from jax.sharding import PartitionSpec as P

Z = 16
LANES = 4
TP = 8
PLANE = LANES * TP
DH = 128
P_SIZE = 64
SPAN = 256
KEYS = 1024
ROWS = 1024
UNIT = 256
REACH = 4
ROUNDS = 4
SCALE = 128.0 ** -0.5
LOW = -1e30
MESH = pl.DeviceIdType.MESH
F32 = jnp.float32
BF16 = jnp.bfloat16


def dot(a, b, ca, cb):
    return lax.dot_general(a, b, (((ca,), (cb,)), ((), ())), preferred_element_type=F32)


def in_weights(decay):
    u = 2.0 * decay
    series = 1.0 + u * (1.0 / 12)
    for k in range(11, 1, -1):
        series = 1.0 + u * (1.0 / k) * series
    return jnp.sqrt(jnp.where(u < -1.0, 1.0 - jnp.exp(u), -u * series))


def kernel(
    length_ref, start_ref, skip_ref,
    q_hbm, k_hbm, v_hbm, x_hbm, dec_hbm, b_hbm, c_hbm, kc_hbm, vc_hbm, init_hbm, norm_hbm, gate_hbm,
    attn_ref, ssm_ref,
    q_ref, k_ref, v_ref, x_ref, dec_ref, b_ref, c_ref, kc_ref, vc_ref, init_ref, gain_ref, gate_ref,
    a_send, a_recv, q_send, q_recv, kv_send, kv_recv, g_recv, cache, fresh,
    p1_send, p1_recv, p2_send, p2_recv, p3_send, p3_recv,
    cum_ref, y_ref, gates, direct, o1, m1, l1, o_send, o_recv, y_send, y_recv,
    in_sem, a_sem, q_sem, kv_sem, g_sem, z_ss, z_rs, p1_sem, p2_ss, p2_rs, p3_sem, o_sem, y_sem, ready,
):
    seq, tp = lax.axis_index("seq"), lax.axis_index("tp")
    z, lane = seq // LANES, lax.rem(seq, LANES)
    me = lane * TP + tp
    four, member = z // 4, lax.rem(z, 4)

    loads = [
        pltpu.make_async_copy(src, dst, in_sem.at[n])
        for n, (src, dst) in enumerate(
            (
                (x_hbm, x_ref), (b_hbm, b_ref), (c_hbm, c_ref), (dec_hbm, dec_ref),
                (k_hbm, k_ref), (v_hbm, v_ref), (kc_hbm, kc_ref), (vc_hbm, vc_ref),
                (q_hbm, q_ref), (norm_hbm, gain_ref.at[pl.ds(0, 8)]),
                (init_hbm.at[lane * 4 + member], init_ref), (gate_hbm, gate_ref),
            )
        )
    ]
    for load in loads:
        load.start()
    fresh[...] = jnp.zeros_like(fresh)

    def place(d):
        return (z * LANES + d // TP, lax.rem(d, TP))

    def along(k):
        return (lax.rem(z + Z + k, Z) * LANES + lane, tp)

    barrier = pltpu.get_barrier_semaphore()

    def greet(i, unused):
        pl.semaphore_signal(
            barrier, inc=1, device_id=place(lax.rem(me + i, PLANE)), device_id_type=MESH
        )
        return unused

    offsets = [k for k in range(-REACH, REACH + 1) if k]
    for k in offsets:
        pl.semaphore_signal(barrier, inc=1, device_id=along(k), device_id_type=MESH)
    lax.fori_loop(1, PLANE, greet, 0)
    early = z < Z // 2

    @pl.when(early)
    def greet_far():
        pl.semaphore_signal(barrier, inc=1, device_id=along(8), device_id_type=MESH)


    for load in loads[:8]:
        load.wait()
    cache[z, 0:64, :] = kc_ref[...]
    cache[z, 64:128, :] = vc_ref[...]
    xx = x_ref[...].astype(F32)
    dec = dec_ref[...].astype(F32)
    bb = b_ref[...].astype(F32)
    cc = c_ref[...].astype(F32)
    kk = k_ref[...].astype(F32)
    vv = v_ref[...].astype(F32)

    def columns(a, first, count):
        return jnp.concatenate(
            [a[:, (first + j) * 128:(first + j + 1) * 128] for j in range(count)], 0
        ).astype(BF16)

    place_at = (seq * TP + tp) * 8 + lax.broadcasted_iota(jnp.int32, (8, 128), 0)
    dec = jnp.where(place_at >= start_ref[0], dec, 0.0)
    dec_block = jnp.concatenate([dec, in_weights(dec)], 0).astype(BF16)
    for t in range(TP):
        at = slice(t * 128, (t + 1) * 128)
        bc_block = jnp.concatenate([bb[:, at], cc[:, at]], 0).astype(BF16)
        kv_send[t] = jnp.concatenate([kk[:, at], vv[:, at]], 0).astype(BF16)
        for l in range(LANES):
            d = l * TP + t
            a_send[d, 0:16, :] = columns(xx, t * 8 + l * 2, 2)
            a_send[d, 16:32, :] = bc_block
            a_send[d, 32:48, :] = dec_block
    a_recv[me] = a_send[me]
    kv_recv[tp] = kv_send[tp]
    for load in loads[8:10]:
        load.wait()
    qq = q_ref[...].astype(F32)
    for t in range(TP):
        q_send[t] = columns(qq, t * 4, 4)
    q_recv[me] = q_send[tp]
    tile_row = lax.broadcasted_iota(jnp.int32, (8, 128), 0)
    tile_lane = lax.broadcasted_iota(jnp.int32, (8, 128), 1)
    skips = jnp.zeros((8, 128), F32)
    for h in range(16):
        skips = jnp.where(tile_row * 2 + tile_lane // P_SIZE == h, skip_ref[h], skips)
    gain_ref[8:16, :] = skips
    g_recv[tp] = gain_ref[...]
    pl.semaphore_wait(barrier, PLANE - 1 + len(offsets) + jnp.where(early, 0, 1))

    @pl.when(z >= Z // 2)
    def answer():
        pl.semaphore_signal(ready, inc=1, device_id=along(8), device_id_type=MESH)


    def copy(src, dst, send, recv, device):
        return pltpu.make_async_remote_copy(
            src_ref=src, dst_ref=dst, send_sem=send, recv_sem=recv,
            device_id=device, device_id_type=MESH,
        )

    def kv_copy(t, slot):
        return copy(kv_send.at[t], kv_recv.at[slot], kv_sem.at[0], kv_sem.at[1], (seq, t))

    def g_copy(t, slot):
        return copy(gain_ref, g_recv.at[slot], g_sem.at[0], g_sem.at[1], (seq, t))

    def a_copy(d, slot):
        return copy(a_send.at[d], a_recv.at[slot], a_sem.at[0], a_sem.at[1], place(d))

    def q_copy(d, slot):
        return copy(
            q_send.at[lax.rem(d, TP)], q_recv.at[slot], q_sem.at[0], q_sem.at[1], place(d)
        )

    def o_copy(d, slot):
        return copy(o_send.at[d], o_recv.at[slot], o_sem.at[0], o_sem.at[1], place(d))

    def y_copy(d, slot):
        return copy(y_send.at[d], y_recv.at[slot], y_sem.at[0], y_sem.at[1], place(d))

    def settle(buf, sem, count):
        part = buf.at[pl.ds(0, count)]
        pltpu.make_async_copy(part, part, sem).wait()

    def over_plane(act):
        def body(i, unused):
            act(lax.rem(me + i, PLANE))
            return unused

        lax.fori_loop(1, PLANE, body, 0)

    def over_tp(act):
        def body(i, unused):
            act(lax.rem(tp + i, TP))
            return unused

        lax.fori_loop(1, TP, body, 0)

    def hop(buf, ring, from_block, k, mark):
        block = lax.rem(z + Z + from_block, Z)
        return copy(
            buf.at[block], buf.at[block], z_ss.at[ring, mark], z_rs.at[ring, block], along(k)
        )

    def landed(buf, ring, k):
        hop(buf, ring, k, 1, 0).wait_recv()

    def wrapped(k):
        return lax.rem(z + Z + k, Z)

    def ups(r):
        return [(-2 * r, k, 2 * r + k - 1, (z >= 2 * r) & (z + k < Z)) for k in (2, 1)]

    def downs(r):
        block = wrapped(2 * r)
        return [
            (2 * r, -k, 7 + 2 * r + k, block <= (6 if k == 2 else 2 * r))
            for k in ((2, 1) if r < ROUNDS - 1 else (1,))
        ]

    hops = [one for r in range(ROUNDS) for one in ups(r) + downs(r)]

    def launch(buf, ring, which, causal):
        for from_block, k, mark, needed in which:
            if causal:
                pl.when(needed)(lambda f=from_block, k=k, m=mark: hop(buf, ring, f, k, m).start())
            else:
                hop(buf, ring, from_block, k, mark).start()

    def arrive(buf, ring, k, causal):
        if causal:
            block = wrapped(k)
            pl.when(block <= 6 if k in (2, 4, 6) else block < z)(lambda: landed(buf, ring, k))
        else:
            landed(buf, ring, k)

    def begin(buf, ring, causal):
        launch(buf, ring, ups(0) + downs(0), causal)

    def forward(buf, ring, r, causal):
        arrive(buf, ring, -2 * r, causal)
        launch(buf, ring, ups(r), causal)
        arrive(buf, ring, 2 * r, causal)
        launch(buf, ring, downs(r), causal)

    def sent(buf, ring, causal):
        for from_block, k, mark, needed in hops:
            if causal:
                pl.when(needed)(
                    lambda f=from_block, k=k, m=mark: hop(buf, ring, f, k, m).wait_send()
                )
            else:
                hop(buf, ring, from_block, k, mark).wait_send()

    others = (-1, 1, -3, 3, -5, 5, -7, 7, 8)

    over_tp(lambda t: kv_copy(t, tp).start())
    begin(cache, 0, False)
    over_plane(lambda d: a_copy(d, me).start())
    over_plane(lambda d: q_copy(d, me).start())
    over_tp(lambda t: g_copy(t, tp).start())

    forward(cache, 0, 1, False)

    settle(kv_recv, kv_sem.at[1], TP - 1)
    kv = kv_recv[...].astype(F32)
    fresh[z, 0:64, :] = kv[:, 0:8, :].reshape(64, DH).astype(BF16)
    fresh[z, 64:128, :] = kv[:, 8:16, :].reshape(64, DH).astype(BF16)
    begin(fresh, 1, True)
    forward(cache, 0, 2, False)
    row = lax.broadcasted_iota(jnp.int32, (SPAN, SPAN), 0)
    col = lax.broadcasted_iota(jnp.int32, (SPAN, SPAN), 1)
    lower = row >= col
    ones = lower.astype(F32).astype(BF16)
    mine = (
        lax.broadcasted_iota(jnp.int32, (128, SPAN), 0)
        == tp * 16 + lane * 4 + lax.broadcasted_iota(jnp.int32, (128, SPAN), 1) // P_SIZE
    )
    mine = mine.astype(F32).astype(BF16)
    forward(fresh, 1, 1, True)
    settle(a_recv, a_sem.at[1], PLANE - 1)

    def halves(first_row):
        part = a_recv[:, first_row:first_row + 16, :].astype(F32)
        return part[:, 0:8, :].reshape(SPAN, 128), part[:, 8:16, :].reshape(SPAN, 128)

    b_all, c_all = halves(16)
    b_all, c_all = b_all.astype(BF16), c_all.astype(BF16)
    decays, weights = halves(32)
    d_all = dot(decays.astype(BF16), mine, 1, 0).astype(BF16)
    x_all = jnp.concatenate(halves(0), 1) * dot(weights.astype(BF16), mine, 1, 0)
    cum = dot(ones, d_all, 1, 0)
    end = cum[SPAN - 1:SPAN, :]
    local = dot((x_all * jnp.exp(end - cum)).astype(BF16), b_all, 0, 0).astype(BF16)

    def log_rows(log):
        high = log.astype(BF16).astype(F32)
        return jnp.concatenate(
            [jnp.broadcast_to(high, (8, 128)), jnp.broadcast_to(log - high, (8, 128))], 0
        ).astype(BF16)

    for h in range(4):
        p1_send[h, 0:64, :] = local[h * P_SIZE:(h + 1) * P_SIZE, :]
        p1_send[h, 64:80, :] = log_rows(
            jnp.broadcast_to(end[:, h * P_SIZE:h * P_SIZE + 1], (1, 128))
        )
    p1_recv[member] = p1_send[member]

    def peer(k):
        return lax.rem(member + k, 4)

    def in_four(m):
        return ((four * 4 + m) * LANES + lane, tp)

    def p1_copy(m, slot):
        return copy(p1_send.at[m], p1_recv.at[slot], p1_sem.at[0], p1_sem.at[1], in_four(m))

    def p2_copy(f, slot):
        return copy(
            p2_send, p2_recv.at[slot], p2_ss.at[f], p2_rs.at[slot],
            ((f * 4 + member) * LANES + lane, tp),
        )

    def p3_copy(m, slot):
        return copy(p3_send.at[m], p3_recv.at[slot], p3_sem.at[0], p3_sem.at[1], in_four(m))

    for k in (1, 2, 3):
        p1_copy(peer(k), member).start()
    cum_ref[...] = cum
    forward(cache, 0, 3, False)

    x_all = x_all.astype(BF16)
    cum_t = dot(d_all, ones, 0, 1)
    pair = dot(c_all, b_all, 1, 1)
    first_half = lax.broadcasted_iota(jnp.int32, (SPAN, 128), 1) < P_SIZE
    for half in range(2):
        parts = []
        for j in (2 * half, 2 * half + 1):
            gap = cum[:, j * P_SIZE:j * P_SIZE + 1] - cum_t[j * P_SIZE:j * P_SIZE + 1, :]
            fade = jnp.where(lower, jnp.exp(jnp.where(lower, gap, 0.0)), 0.0)
            parts.append(
                dot((pair * fade).astype(BF16), x_all[:, half * 128:(half + 1) * 128], 1, 0)
            )
        y_ref[:, half * 128:(half + 1) * 128] = jnp.where(first_half, parts[0], parts[1])

    forward(fresh, 1, 2, True)

    settle(p1_recv, p1_sem.at[1], 3)

    def state_of(tile):
        tail = tile[64:80, :].astype(F32)
        return tile[0:64, :].astype(F32), tail[0:1, :] + tail[8:9, :]

    steps = [state_of(p1_recv[m]) for m in range(4)]
    total, total_log = steps[0]
    for add, log in steps[1:]:
        total, total_log = total * jnp.exp(log) + add, total_log + log
    p2_send[0:64, :] = total.astype(BF16)
    p2_send[64:80, :] = log_rows(total_log)
    pl.when(early)(lambda: pl.semaphore_wait(ready, 1))
    for k in (1, 2, 3):
        pl.when(four + k < 4)(lambda k=k: p2_copy(four + k, four).start())

    def spread():
        for k in (1, 2, 3):
            pl.when(four - k >= 0)(lambda k=k: p2_copy(four, four - k).wait_recv())

        def lap(f, prior):
            add, log = state_of(p2_recv[f])
            return prior * jnp.exp(log) + add

        prior = lax.fori_loop(0, four, lap, init_ref[...])
        for m in range(4):
            p3_send[m] = prior.astype(BF16)
            if m < 3:
                add, log = state_of(p1_recv[m])
                prior = prior * jnp.exp(log) + add
        p3_recv[member] = p3_send[member]
        for k in (1, 2, 3):
            p3_copy(peer(k), member).start()

    loads[10].wait()
    pl.when(four == 0)(spread)

    key_at = lax.broadcasted_iota(jnp.int32, (1, KEYS), 1)
    key_place = (key_at // 64) * SPAN + lane * 64 + lax.rem(key_at, 64)
    row_at = lax.broadcasted_iota(jnp.int32, (UNIT, 1), 0)

    def part(u, buf, usable, blocks=Z):
        queries = q_recv[pl.ds(u * 8, 8)].reshape(UNIT, DH)
        keys = buf[0:blocks, 0:64, :].reshape(blocks * 64, DH)
        values = buf[0:blocks, 64:128, :].reshape(blocks * 64, DH)
        scores = jnp.where(usable, dot(queries, keys, 1, 1) * SCALE, LOW)
        top = jnp.max(scores, axis=1, keepdims=True)
        weights = jnp.exp(scores - top)
        total = jnp.sum(weights, axis=1, keepdims=True)
        return top, total, dot(weights.astype(BF16), values, 1, 0)

    settle(q_recv, q_sem.at[1], PLANE - 1)
    for k in others:
        arrive(cache, 0, k, False)
    cached = key_place < length_ref[0]
    for u in range(ROWS // UNIT):
        top, weight, mixed = part(u, cache, cached)
        m1[u * UNIT:(u + 1) * UNIT, :] = top
        l1[u * UNIT:(u + 1) * UNIT, :] = weight
        o1[u * UNIT:(u + 1) * UNIT, :] = mixed
        if u == 1:
            forward(fresh, 1, 3, True)

    pl.when(four > 0)(spread)

    for k in others:
        arrive(fresh, 1, k, True)
    spot = (
        lax.broadcasted_iota(jnp.int32, (1, 32, 128), 1)
        == lax.broadcasted_iota(jnp.int32, (1, 32, 128), 2)
    ).astype(F32)
    spot_row = lax.broadcasted_iota(jnp.int32, (8, 16, 128), 1)

    def unit(i, blocks):
        u = lax.rem(lane + 1 + i, LANES)
        query_place = z * SPAN + u * 64 + (row_at // 32) * 8 + lax.rem(row_at, 8)
        places = key_place[:, 0:blocks * 64]
        usable = (places >= start_ref[0]) & (places <= query_place)
        top, weight, mixed = part(u, fresh, usable, blocks)
        rows = pl.ds(pl.multiple_of(u * UNIT, UNIT), UNIT)
        top1, weight1 = m1[rows, :], l1[rows, :]
        both = jnp.maximum(top, top1)
        by, by1 = jnp.exp(top - both), jnp.exp(top1 - both)
        weight = weight * by + weight1 * by1
        mixed = (mixed * by + o1[rows, :] * by1) / weight
        o_send[pl.ds(u * 8, 8), 0:32, :] = mixed.astype(BF16).reshape(8, 32, DH)
        size = jnp.broadcast_to(both + jnp.log(weight), (UNIT, 128)).reshape(8, 32, 128)
        size = jnp.sum(size * spot, axis=1, keepdims=True)
        high = size.astype(BF16).astype(F32)
        middle = (size - high).astype(BF16).astype(F32)
        o_send[pl.ds(u * 8, 8), 32:48, :] = jnp.where(
            spot_row < 8, high, jnp.where(spot_row < 15, middle, size - high - middle)
        ).astype(BF16)
        for n in range(1, TP):
            o_copy(u * TP + lax.rem(tp + n, TP), me).start()
        pl.when(u != lane)(lambda: o_copy(u * TP + tp, me).start())

    def units(blocks):
        for i in range(LANES):
            unit(i, blocks)

    pl.when(z < Z // 2)(lambda: units(Z // 2))
    pl.when(z >= Z // 2)(lambda: units(Z))
    o_recv[me] = o_send[me]

    settle(p3_recv, p3_sem.at[1], 3)
    incoming = p3_recv[...].reshape(SPAN, 128)
    y = y_ref[...] + jnp.exp(cum_ref[...]) * dot(c_all, incoming, 1, 1)
    y_send[...] = jnp.concatenate(
        [y[:, 0:128].reshape(PLANE, 8, 128), y[:, 128:256].reshape(PLANE, 8, 128)], 1
    ).astype(BF16)
    y_recv[me] = y_send[me]
    over_plane(lambda d: y_copy(d, me).start())

    settle(g_recv, g_sem.at[1], TP - 1)
    loads[11].wait()
    for t in range(TP):
        for r in range(8):
            at = slice(t * 1024 + r * 128, t * 1024 + (r + 1) * 128)
            gate = gate_ref[:, at].astype(F32)
            gates[:, at] = gate / (1.0 + jnp.exp(-gate))
            direct[:, at] = g_recv[t, 8 + r:9 + r, :] * x_ref[:, at].astype(F32)
    settle(o_recv, o_sem.at[1], PLANE - 1)
    for t in range(TP):
        sizes = []
        for l in range(LANES):
            tile = o_recv[l * TP + t, 32:48, :].astype(F32)
            line = tile[0:1, :] + tile[8:9, :] + tile[15:16, :]
            sizes.append(jnp.sum(line * spot[0], axis=1, keepdims=True))
        most = jnp.maximum(jnp.maximum(sizes[0], sizes[1]), jnp.maximum(sizes[2], sizes[3]))
        shares = [jnp.exp(size - most) for size in sizes]
        whole = shares[0] + shares[1] + shares[2] + shares[3]
        out = sum(
            share * o_recv[l * TP + t, 0:32, :].astype(F32) for l, share in enumerate(shares)
        ) / whole
        for h in range(4):
            at = (t * 4 + h) * 128
            attn_ref[:, at:at + 128] = out[h * 8:(h + 1) * 8, :].astype(BF16)

    settle(y_recv, y_sem.at[1], PLANE - 1)
    for t in range(TP):
        gated, squares = [], 0.0
        for l in range(LANES):
            y_part = y_recv[l * TP + t].astype(F32)
            for half in range(2):
                r = l * 2 + half
                at = t * 1024 + r * 128
                value = y_part[half * 8:(half + 1) * 8, :] + direct[:, at:at + 128]
                value = value * gates[:, at:at + 128]
                squares = squares + value * value
                gated.append(value)
        scale = lax.rsqrt(jnp.sum(squares, axis=1, keepdims=True) * (1.0 / 1024) + 1e-5)
        for r in range(8):
            at = t * 1024 + r * 128
            ssm_ref[:, at:at + 128] = (gated[r] * scale * g_recv[t, r:r + 1, :]).astype(BF16)

    settle(kv_recv, kv_sem.at[0], TP - 1)
    settle(g_recv, g_sem.at[0], TP - 1)
    settle(a_recv, a_sem.at[0], PLANE - 1)
    settle(q_recv, q_sem.at[0], PLANE - 1)
    settle(o_recv, o_sem.at[0], PLANE - 1)
    settle(y_recv, y_sem.at[0], PLANE - 1)
    settle(p1_recv, p1_sem.at[0], 3)
    settle(p3_recv, p3_sem.at[0], 3)
    sent(cache, 0, False)
    sent(fresh, 1, True)
    for k in (1, 2, 3):
        pl.when(four + k < 4)(lambda k=k: p2_copy(four + k, four).wait_send())


def local(
    query, key_new, value_new, ssm_input, ssm_gate, ssm_b, ssm_c, log_decay,
    key_cache, value_cache, init_state, skip_gain, norm_gain, cache_length, span_start,
):
    vmem = pl.BlockSpec(memory_space=pltpu.VMEM)
    smem = pl.BlockSpec(memory_space=pltpu.SMEM)
    hbm = pl.BlockSpec(memory_space=pltpu.HBM)
    dma = pltpu.SemaphoreType.DMA
    return pl.pallas_call(
        kernel,
        out_shape=(
            pltpu.VMEM((8, 4096), BF16),
            pltpu.VMEM((8, 8192), BF16),
        ),
        in_specs=[smem] * 3 + [hbm] * 12,
        out_specs=(vmem, vmem),
        scratch_shapes=[
            pltpu.VMEM((8, 4096), BF16),
            pltpu.VMEM((8, 1024), BF16),
            pltpu.VMEM((8, 1024), BF16),
            pltpu.VMEM((8, 8192), BF16),
            pltpu.VMEM((8, 128), BF16),
            pltpu.VMEM((8, 1024), BF16),
            pltpu.VMEM((8, 1024), BF16),
            pltpu.VMEM((64, 128), BF16),
            pltpu.VMEM((64, 128), BF16),
            pltpu.VMEM((64, 128), F32),
            pltpu.VMEM((16, 128), F32),
            pltpu.VMEM((8, 8192), BF16),
            pltpu.VMEM((PLANE, 48, 128), BF16),
            pltpu.VMEM((PLANE, 48, 128), BF16),
            pltpu.VMEM((TP, 32, 128), BF16),
            pltpu.VMEM((PLANE, 32, 128), BF16),
            pltpu.VMEM((TP, 16, 128), BF16),
            pltpu.VMEM((TP, 16, 128), BF16),
            pltpu.VMEM((TP, 16, 128), F32),
            pltpu.VMEM((Z, 128, DH), BF16),
            pltpu.VMEM((Z, 128, DH), BF16),
            pltpu.VMEM((4, 80, 128), BF16),
            pltpu.VMEM((4, 80, 128), BF16),
            pltpu.VMEM((80, 128), BF16),
            pltpu.VMEM((4, 80, 128), BF16),
            pltpu.VMEM((4, 64, 128), BF16),
            pltpu.VMEM((4, 64, 128), BF16),
            pltpu.VMEM((SPAN, SPAN), F32),
            pltpu.VMEM((SPAN, SPAN), F32),
            pltpu.VMEM((8, 8192), F32),
            pltpu.VMEM((8, 8192), F32),
            pltpu.VMEM((ROWS, DH), F32),
            pltpu.VMEM((ROWS, 1), F32),
            pltpu.VMEM((ROWS, 1), F32),
            pltpu.VMEM((PLANE, 48, 128), BF16),
            pltpu.VMEM((PLANE, 48, 128), BF16),
            pltpu.VMEM((PLANE, 16, 128), BF16),
            pltpu.VMEM((PLANE, 16, 128), BF16),
            dma((12,)), dma((2,)), dma((2,)), dma((2,)), dma((2,)),
            dma((2, 16)), dma((2, Z)),
            dma((2,)), dma((4,)), dma((4,)), dma((2,)), dma((2,)), dma((2,)),
            pltpu.SemaphoreType.REGULAR,
        ],
        compiler_params=pltpu.CompilerParams(
            collective_id=0, has_side_effects=True, vmem_limit_bytes=56 * 1024 * 1024
        ),
        name="mixers",
    )(
        cache_length, span_start, skip_gain,
        query, key_new, value_new, ssm_input, log_decay, ssm_b, ssm_c,
        key_cache, value_cache, init_state, norm_gain.reshape(8, 128), ssm_gate,
    )


def solution(mesh):
    rows = P(("seq", "tp"), None)
    placed = (rows,) * 8 + (
        P("seq", "tp"),
        P("seq", "tp"),
        P("tp", None, None),
        P("tp"),
        P("tp"),
        P(),
        P(),
    )
    return jax.shard_map(
        local, mesh=mesh, in_specs=placed, out_specs=(rows, rows), check_vma=False
    )
```
